768 devices in a mesh: vocab: 16 (over z_hi, x), dp: 48 (over z_lo, y, core).
Axes of the slice: x: 4, y: 8, z: 12 (z_hi: 4, z_lo: 3; z = z_hi * 3 + z_lo), core: 2. Of those that a mesh axis runs over, the one named last changes fastest.
Arguments:
- hidden: bfloat16 [30720, 2048], P('dp'), may hold values from -300 to 300
- head: bfloat16 [13824, 2048], P('vocab'), may hold values from -1 to 1
- targets: int32 [30720], P('dp'), may hold values from 0 to 13823
- mask_counts: int32 [192], P('dp'), may hold values from 20 to 160, as said below
- answer_lengths: int32 [192], P('dp'), may hold values from 20 to 640, as said below
Outputs:
- seq_loss: float32 [192], P('dp')
- head_grad: float32 [13824, 2048], P(('vocab', 'dp'))
The draws below stay inside these ranges and needn't reach their ends.
Inputs may be any that keep to these rules, and one draw needn't show every extreme that they name: `mask_counts`: in each data group the counts sum to at most 640; in every draw some data group has all its counts equal to 160. `answer_lengths`: each sequence's length is at least its mask count and at most four times it.
All inputs are finite; a program needn't handle non-finite values.
Results may differ from the reference program's by a relative error of at most 0.0025.
Values sent between devices are 32-bit elements; how exact they have to be, the bound alone decides.
A program may use at most 64 MiB of HBM per device.

```python
import jax
import jax.numpy as jnp
from jax import lax

D = 2048
ROWS = 640
SEQS = 4
VOCAB = 13824
ALLROWS = 30720
N_DP = 48


def counts_and_lengths(key):
    key_counts, key_full, key_extra = jax.random.split(key, 3)
    lowest = ROWS // (8 * SEQS)
    highest = ROWS // SEQS
    counts = jax.random.randint(key_counts, (N_DP, SEQS), lowest, highest + 1)
    full_group = jax.random.randint(key_full, (), 0, N_DP)
    least_group = (full_group + 1) % N_DP
    group_ids = jnp.arange(N_DP, dtype=jnp.int32)[:, None]
    seq_ids = jnp.arange(SEQS, dtype=jnp.int32)[None, :]
    counts = jnp.where(group_ids == full_group, highest, counts)
    least_slot = (group_ids == least_group) & (seq_ids == 0)
    counts = jnp.where(least_slot, lowest, counts)
    extra = jax.random.randint(key_extra, (N_DP, SEQS), 0, 3 * counts + 1)
    extra = jnp.where(least_slot, 0, extra)
    lengths = counts + extra
    lengths = jnp.where((group_ids == full_group) & (seq_ids == 0), 4 * highest, lengths)
    return (counts.reshape(-1).astype(jnp.int32), lengths.reshape(-1).astype(jnp.int32))


def draw_mask_counts(key, part):
    counts, lengths = counts_and_lengths(key)
    return counts


def draw_answer_lengths(key, part):
    counts, lengths = counts_and_lengths(key)
    return lengths


def draw_head(key, part):
    key = jax.random.fold_in(key, 11)
    key_base = jax.random.fold_in(key, 0)
    base = jax.random.normal(key_base, (VOCAB, D), jnp.float32) * (1.0 / D ** 0.5)
    return jnp.clip(base, -1.0, 1.0).astype(jnp.bfloat16)


def draw_hidden(key, part):
    key = jax.random.fold_in(key, 7)
    key_noise, key_scale = jax.random.split(key, 2)
    noise = jax.random.normal(key_noise, (ALLROWS, D), jnp.float32)
    spread = jax.random.uniform(key_scale, (ALLROWS, 1), jnp.float32)
    scales = jnp.exp(jnp.log(0.5) + spread * jnp.log(8.0))
    values = scales * noise
    return jnp.clip(values, -300.0, 300.0).astype(jnp.bfloat16)


def place_ends(values, stream_key, low, largest):
    shape = values.shape
    place = [jax.random.randint(jax.random.fold_in(stream_key, axis), (), 0, shape[axis]) for axis in range(len(shape))]
    values = values.at[tuple(place)].set(low)
    longest = shape.index(max(shape))
    place[longest] = (place[longest] + 1) % shape[longest]
    return values.at[tuple(place)].set(largest)


def setup_inputs(seed: int = 0) -> dict:
    splits = jax.random.split(jax.random.key(seed), 6)
    return {
        "hidden": draw_hidden(jax.random.fold_in(splits[5], 71), 0),
        "head": draw_head(jax.random.fold_in(splits[5], 71), 0),
        "targets": place_ends(jax.random.randint(splits[2], (ALLROWS,), 0, VOCAB), jax.random.fold_in(splits[2], 1), 0, VOCAB - 1).astype(jnp.int32),
        "mask_counts": draw_mask_counts(jax.random.fold_in(splits[5], 71), 0),
        "answer_lengths": draw_answer_lengths(jax.random.fold_in(splits[5], 71), 0),
    }


def row_weights(counts, lengths, row_count):
    position = jnp.arange(row_count, dtype=jnp.int32)
    seq_ends = jnp.cumsum(counts).astype(jnp.int32)
    member = jnp.sum((position[None, :] >= seq_ends[:, None]).astype(jnp.int32), axis=0)
    onehot_seq = (member[None, :] == jnp.arange(counts.shape[0], dtype=jnp.int32)[:, None]).astype(jnp.float32)
    inverse_rate = lengths.astype(jnp.float32) / counts.astype(jnp.float32)
    weights = jnp.dot(inverse_rate, onehot_seq, precision=lax.Precision.HIGHEST)
    return onehot_seq, weights


def reference(hidden, head, targets, mask_counts, answer_lengths):
    grouped_hidden = hidden.reshape(N_DP, ROWS, D)
    grouped_targets = targets.reshape(N_DP, ROWS)
    grouped_counts = mask_counts.reshape(N_DP, SEQS)
    grouped_lengths = answer_lengths.reshape(N_DP, SEQS)
    vocab_ids = jnp.arange(VOCAB, dtype=jnp.int32)

    def group_step(total, inputs):
        rows_hidden, rows_target, group_counts, group_lengths = inputs
        logits = jnp.dot(rows_hidden, head.T, preferred_element_type=jnp.float32)
        peak = jnp.max(logits, axis=1)
        total_exp = jnp.sum(jnp.exp(logits - peak[:, None]), axis=1)
        log_total = peak + jnp.log(total_exp)
        target_hit = rows_target[:, None] == vocab_ids[None, :]
        target_logit = jnp.sum(jnp.where(target_hit, logits, jnp.float32(0.0)), axis=1)
        cross = log_total - target_logit
        onehot_seq, weights = row_weights(group_counts, group_lengths, ROWS)
        seq_loss = jnp.dot(onehot_seq, cross, precision=lax.Precision.HIGHEST) / group_counts.astype(jnp.float32)
        probability = jnp.exp(logits - log_total[:, None])
        grad_rows = ((probability - target_hit.astype(jnp.float32)) * weights[:, None]).astype(jnp.bfloat16)
        total = total + jnp.dot(grad_rows.T, rows_hidden, preferred_element_type=jnp.float32)
        return total, seq_loss

    start = jnp.zeros((VOCAB, D), jnp.float32)
    head_grad, seq_losses = lax.scan(group_step, start, (grouped_hidden, grouped_targets, grouped_counts, grouped_lengths))
    return seq_losses.reshape(-1), head_grad
```

```python
import jax
import jax.numpy as jnp
from jax import lax
from jax.experimental import pallas as pl
from jax.experimental.pallas import tpu as pltpu
from jax.sharding import PartitionSpec as P

MESH = pl.DeviceIdType.MESH
F32 = jnp.float32

VOCAB_DEVS = 16
NZ, NY, NC = 3, 8, 2
LANES = 128
ROWS_A = 176
DISTANCES = (4, 3, 5, 2, 6, 1, 7, 0)


def kernel(hidden, head, targets, counts, lengths, out, loss,
           logits, probs, grad, stats, hits,
           core_in, ya0, ya, za, yb0, yb, zb, last,
           lse_s, lse_r, hit_s, hit_r, core_s, core_r,
           ya_s, ya_r, za_s, za_r, yb_s, yb_r, zb_s, zb_r):
    vocab_rows, width = head.shape
    slots = hidden.shape[0]
    block = vocab_rows * width // LANES // (NZ * NY * NC)
    pitch = width // LANES
    rows_b = block - ROWS_A
    half_a, half_b = ROWS_A // 2, rows_b // 2

    v = lax.axis_index("vocab")
    d = lax.axis_index("dp")
    c = d % NC
    y = (d // NC) % NY
    z = d // (NC * NY)

    partner = d + 1 - 2 * c
    y_next = [(z * NY + (y + 1) % NY) * NC + c, (z * NY + (y + NY - 1) % NY) * NC + c]
    z_peer = [(((z + k) % NZ) * NY + y) * NC + c for k in (1, 2)]
    v_peer = [(v + s) % VOCAB_DEVS for s in range(1, VOCAB_DEVS)]

    barrier = pltpu.get_barrier_semaphore()
    for peer in v_peer:
        pl.semaphore_signal(barrier, inc=1, device_id={"vocab": peer}, device_id_type=MESH)
    for peer in [partner] + y_next + z_peer:
        pl.semaphore_signal(barrier, inc=1, device_id={"dp": peer}, device_id_type=MESH)

    position = lax.broadcasted_iota(jnp.int32, (1, slots), 1)
    seqs = counts.shape[0]
    member = []
    begin = jnp.int32(0)
    weight = jnp.zeros((1, slots), F32)
    for k in range(seqs):
        end = begin + counts[k]
        inside = (position >= begin) & (position < end)
        member.append(inside)
        rate = jnp.full((1, slots), lengths[k], jnp.int32).astype(F32) / jnp.full(
            (1, slots), counts[k], jnp.int32
        ).astype(F32)
        weight = jnp.where(inside, rate, weight)
        begin = end

    part = vocab_rows // 3

    @pl.loop(0, 3)
    def _(i):
        rows = pl.ds(pl.multiple_of(i * part, part), part)
        logits[rows, :] = lax.dot_general(
            head[rows, :], hidden[...], (((1,), (1,)), ((), ())), preferred_element_type=F32
        )

    relative = targets[...] - v * vocab_rows
    tile = 96
    peak = jnp.full((8, slots), -jnp.inf, F32)
    target_sum = jnp.zeros((8, slots), F32)

    def first_pass(i, carry):
        peak, total = carry
        for k in range(tile // 8):
            at = pl.multiple_of(i * tile + k * 8, 8)
            value = logits[pl.ds(at, 8), :]
            ids = lax.broadcasted_iota(jnp.int32, (8, slots), 0) + at
            peak = jnp.maximum(peak, value)
            total = total + jnp.where(ids == relative, value, 0.0)
        return peak, total

    peak, target_sum = lax.fori_loop(0, vocab_rows // tile, first_pass, (peak, target_sum))
    peak = jnp.max(peak, axis=0, keepdims=True)
    hits[0] = jnp.sum(target_sum, axis=0, keepdims=True)

    def second_pass(i, total):
        for k in range(tile // 8):
            at = pl.multiple_of(i * tile + k * 8, 8)
            value = jnp.exp(logits[pl.ds(at, 8), :] - peak)
            logits[pl.ds(at, 8), :] = value
            total = total + value
        return total

    exp_sum = lax.fori_loop(0, vocab_rows // tile, second_pass, jnp.zeros((8, slots), F32))
    own_lse = peak + jnp.log(jnp.sum(exp_sum, axis=0, keepdims=True))
    stats[0] = own_lse

    pl.semaphore_wait(barrier, VOCAB_DEVS - 1 + 1 + 2 + 2)

    waits = []

    def send(src, dst, send_sem, recv_sem, axis, peer):
        copy = pltpu.make_async_remote_copy(
            src_ref=src, dst_ref=dst, send_sem=send_sem, recv_sem=recv_sem,
            device_id={axis: peer}, device_id_type=MESH,
        )
        copy.start()
        waits.append(copy)
        return copy

    lse_copies = [
        send(stats.at[0], stats.at[s], lse_s.at[s], lse_r.at[s], "vocab", v_peer[s - 1])
        for s in range(1, VOCAB_DEVS)
    ]
    hit_copies = [
        send(hits.at[0], hits.at[s], hit_s.at[s], hit_r.at[s], "vocab", v_peer[s - 1])
        for s in range(1, VOCAB_DEVS)
    ]
    for copy in lse_copies:
        copy.wait_recv()
    top = own_lse
    for s in range(1, VOCAB_DEVS):
        top = jnp.maximum(top, stats[s])
    total = jnp.exp(own_lse - top)
    for s in range(1, VOCAB_DEVS):
        total = total + jnp.exp(stats[s] - top)
    log_total = top + jnp.log(total)

    shift = jnp.exp(peak - log_total)

    @pl.loop(0, vocab_rows // 48)
    def _(i):
        for k in range(3):
            at = pl.multiple_of(i * 48 + k * 16, 16)
            ids = lax.broadcasted_iota(jnp.int32, (16, slots), 0) + at
            onehot = jnp.where(ids == relative, 1.0, 0.0)
            value = (logits[pl.ds(at, 16), :] * shift - onehot) * weight
            probs[pl.ds(at, 16), :] = value.astype(jnp.bfloat16)

    @pl.loop(0, width // 256)
    def _(n):
        columns = pl.ds(pl.multiple_of(n * 256, 256), 256)
        value = jnp.dot(probs[...], hidden[:, columns], preferred_element_type=F32)
        for j in range(2):
            grad[pl.ds(n * 2 + j, vocab_rows, stride=pitch), :] = value[:, j * LANES:(j + 1) * LANES]

    def line(zo, yo, co):
        return pl.multiple_of(((zo * NY + yo) * NC + co) * block, 8)

    def own(zo, yo, start, count):
        return pl.ds(pl.multiple_of(line(zo, yo, c) + start, 8), count)

    core_copies = {}
    for i, dist in enumerate(DISTANCES):
        yo = (y + dist) % NY
        for zo in range(NZ):
            at = i * NZ + zo
            core_copies[dist, zo] = send(
                grad.at[pl.ds(line(zo, yo, 1 - c), block)], core_in.at[at],
                core_s.at[at], core_r.at[at], "dp", partner,
            )

    zb_copies, ya_copies, yb_copies = {}, {}, {}

    def pair_sum(dist):
        yo = (y + dist) % NY
        i = DISTANCES.index(dist)
        for zo in range(NZ):
            core_copies[dist, zo].wait_recv()
            grad[own(zo, yo, 0, block), :] += core_in[i * NZ + zo]
        for k in range(2):
            zb_copies[dist, k] = send(
                grad.at[own((z + k + 1) % NZ, yo, ROWS_A, rows_b)], zb.at[k, dist],
                zb_s.at[k, dist], zb_r.at[k, dist], "dp", z_peer[k],
            )

    def owner(way, t):
        return (y + (4 - t if way == 0 else 4 + t)) % NY

    def step_a(t):
        if t > 0:
            for zo in range(NZ):
                for way in range(2):
                    ya_copies[way, t - 1, zo].wait_recv()
                    if t == 1:
                        grad[own(zo, owner(way, 1), way * half_a, half_a), :] += ya0[way, zo]
                    else:
                        grad[own(zo, owner(way, t), 0, ROWS_A), :] += ya[way, t - 2, zo]
                    if t < 4:
                        send_a(way, t, zo)
        else:
            for zo in range(NZ):
                for way in range(2):
                    send_a(way, 0, zo)

    def send_a(way, t, zo):
        if t == 0:
            src, dst = own(zo, owner(way, 0), way * half_a, half_a), ya0.at[way, zo]
        else:
            src, dst = own(zo, owner(way, t), 0, ROWS_A), ya.at[way, t - 1, zo]
        ya_copies[way, t, zo] = send(
            grad.at[src], dst, ya_s.at[way, t, zo], ya_r.at[way, t, zo], "dp", y_next[way]
        )

    def z_sum(dist):
        yo = (y + dist) % NY
        for k in range(2):
            zb_copies[dist, k].wait_recv()
        grad[own(z, yo, ROWS_A, rows_b), :] += zb[0, dist] + zb[1, dist]

    def step_b(t):
        for way in range(2):
            if t > 0:
                yb_copies[way, t - 1].wait_recv()
                if t == 1:
                    grad[own(z, owner(way, 1), ROWS_A + way * half_b, half_b), :] += yb0[way]
                else:
                    grad[own(z, owner(way, t), ROWS_A, rows_b), :] += yb[way, t - 2]
            if t == 0:
                src, dst = own(z, owner(way, 0), ROWS_A + way * half_b, half_b), yb0.at[way]
            elif t < 4:
                src, dst = own(z, owner(way, t), ROWS_A, rows_b), yb.at[way, t - 1]
            else:
                continue
            yb_copies[way, t] = send(
                grad.at[src], dst, yb_s.at[way, t], yb_r.at[way, t], "dp", y_next[way]
            )

    pair_sum(4)
    step_a(0)
    pair_sum(3)
    pair_sum(5)
    pair_sum(2)
    step_a(1)
    pair_sum(6)
    pair_sum(1)
    pair_sum(7)
    pair_sum(0)
    z_sum(4)
    step_b(0)
    step_a(2)
    z_sum(3)
    z_sum(5)
    step_b(1)
    step_a(3)
    z_sum(2)
    z_sum(6)
    step_b(2)
    z_sum(1)
    z_sum(7)
    step_b(3)
    step_a(4)
    za_copies = [
        send(grad.at[own((z + k + 1) % NZ, y, 0, ROWS_A)], za.at[k], za_s.at[k], za_r.at[k],
             "dp", z_peer[k])
        for k in range(2)
    ]
    z_sum(0)
    step_b(4)

    for copy in hit_copies:
        copy.wait_recv()
    target_logit = hits[0]
    for s in range(1, VOCAB_DEVS):
        target_logit = target_logit + hits[s]
    cross = log_total - target_logit
    for k in range(seqs):
        mean = jnp.where(member[k], cross, 0.0) / jnp.full((1, slots), counts[k], jnp.int32).astype(F32)
        loss[k] = jnp.sum(mean)

    last[pl.ds(ROWS_A, rows_b), :] = grad[own(z, y, ROWS_A, rows_b), :]
    for copy in za_copies:
        copy.wait_recv()
    last[pl.ds(0, ROWS_A), :] = grad[own(z, y, 0, ROWS_A), :] + za[0] + za[1]
    for j in range(pitch):
        out[:, j * LANES:(j + 1) * LANES] = last[pl.ds(j, out.shape[0], stride=pitch), :]

    for copy in waits:
        copy.wait_send()


def on_device(hidden, head, targets, mask_counts, answer_lengths):
    vocab_rows, width = head.shape
    slots = hidden.shape[0]
    lines = vocab_rows * width // LANES
    block = lines // (NZ * NY * NC)
    rows_b = block - ROWS_A
    vmem = pl.BlockSpec(memory_space=pltpu.VMEM)
    smem = pl.BlockSpec(memory_space=pltpu.SMEM)
    dma = pltpu.SemaphoreType.DMA
    head_grad, seq_loss = pl.pallas_call(
        kernel,
        out_shape=(
            jax.ShapeDtypeStruct((vocab_rows // (NZ * NY * NC), width), F32),
            jax.ShapeDtypeStruct(mask_counts.shape, F32),
        ),
        in_specs=[vmem, vmem, vmem, smem, smem],
        out_specs=(vmem, smem),
        scratch_shapes=[
            pltpu.VMEM((vocab_rows, slots), F32),
            pltpu.VMEM((vocab_rows, slots), jnp.bfloat16),
            pltpu.VMEM((lines, LANES), F32),
            pltpu.VMEM((VOCAB_DEVS, 1, slots), F32),
            pltpu.VMEM((VOCAB_DEVS, 1, slots), F32),
            pltpu.VMEM((NY * NZ, block, LANES), F32),
            pltpu.VMEM((2, NZ, ROWS_A // 2, LANES), F32),
            pltpu.VMEM((2, 3, NZ, ROWS_A, LANES), F32),
            pltpu.VMEM((2, ROWS_A, LANES), F32),
            pltpu.VMEM((2, rows_b // 2, LANES), F32),
            pltpu.VMEM((2, 3, rows_b, LANES), F32),
            pltpu.VMEM((2, NY, rows_b, LANES), F32),
            pltpu.VMEM((block, LANES), F32),
            dma((VOCAB_DEVS,)), dma((VOCAB_DEVS,)),
            dma((VOCAB_DEVS,)), dma((VOCAB_DEVS,)),
            dma((NY * NZ,)), dma((NY * NZ,)),
            dma((2, 4, NZ)), dma((2, 4, NZ)),
            dma((2,)), dma((2,)),
            dma((2, 4)), dma((2, 4)),
            dma((2, NY)), dma((2, NY)),
        ],
        compiler_params=pltpu.CompilerParams(
            collective_id=0, has_side_effects=True, vmem_limit_bytes=48 * 1024 * 1024
        ),
        cost_estimate=pl.CostEstimate(
            flops=4 * vocab_rows * slots * width,
            bytes_accessed=2 * (vocab_rows + slots) * width,
            transcendentals=vocab_rows * slots,
        ),
        name="head_gradient",
    )(hidden, head, targets.reshape(1, slots), mask_counts, answer_lengths)
    return seq_loss, head_grad


def solution(mesh):
    return jax.shard_map(
        on_device,
        mesh=mesh,
        in_specs=(P("dp", None), P("vocab", None), P("dp"), P("dp"), P("dp")),
        out_specs=(P("dp"), P(("vocab", "dp"), None)),
        check_vma=False,
    )
```

```python
import functools

import jax
import jax.numpy as jnp
from jax import lax
from jax.experimental import pallas as pl
from jax.experimental.pallas import tpu as pltpu
from jax.sharding import PartitionSpec as P

MESH = pl.DeviceIdType.MESH
F32 = jnp.float32

NX, NH = 4, 4
NZ, NY, NC = 3, 8, 2
LANES = 128
STEPS = 4
ROWS_A = 176
DISTANCES = (4, 3, 5, 2, 6, 1, 7, 0)


def toward(way, t):
    return (4 - t if way == 0 else 4 + t) % NY


ORDER = (
    ("product", 1), ("swap", 1, 4), ("product", 0), ("pair", 1, 4), ("swap", 0, 4), ("product", 2), ("swap", 2, 4),
    ("swap", 1, 5), ("pair", 0, 4), ("swap", 1, 3), ("swap", 1, 0), ("pair", 2, 4), ("pair", 1, 5), ("swap", 0, 5),
    ("swap", 0, 3), ("swap", 0, 6), ("swap", 0, 1), ("pair", 1, 3), ("a", 1, 1, 0), ("a", 1, 1, 1), ("swap", 2, 5),
    ("swap", 1, 7), ("swap", 2, 2), ("pair", 0, 3), ("a", 0, 1, 0), ("swap", 2, 6), ("swap", 1, 6), ("pair", 0, 5),
    ("swap", 2, 3), ("swap", 1, 1), ("a", 0, 1, 1), ("swap", 0, 7), ("zsum", 4), ("swap", 1, 2), ("pair", 2, 3),
    ("pair", 1, 1), ("pair", 0, 6), ("pair", 1, 6), ("pair", 1, 7), ("pair", 2, 5), ("a", 2, 1, 0), ("a", 2, 1, 1),
    ("swap", 2, 7), ("pair", 1, 2), ("a", 1, 2, 0), ("a", 1, 2, 1), ("pair", 0, 1), ("swap", 0, 0), ("pair", 2, 6),
    ("swap", 2, 1), ("zsum", 3), ("swap", 0, 2), ("pair", 0, 2), ("b", 1, 0), ("zsum", 5), ("pair", 0, 7),
    ("a", 0, 2, 1), ("b", 1, 1), ("a", 0, 2, 0), ("a", 2, 2, 1), ("a", 1, 3, 0), ("a", 1, 3, 1), ("pair", 2, 2),
    ("swap", 2, 0), ("a", 2, 2, 0), ("pair", 1, 0), ("a", 0, 3, 1), ("a", 0, 3, 0), ("zsum", 2), ("pair", 2, 0),
    ("b", 2, 0), ("pair", 2, 1), ("pair", 2, 7), ("pair", 0, 0), ("zsum", 6), ("b", 2, 1), ("zsum", 1),
    ("a", 1, 4, 1), ("zsum", 7), ("a", 1, 4, 0), ("a", 2, 3, 0), ("a", 2, 3, 1), ("a", 0, 4, 1), ("zsum", 0),
    ("a", 0, 4, 0), ("b", 3, 0), ("b", 3, 1), ("a", 2, 4, 0), ("a", 2, 4, 1), ("end",), ("b", 4, 0), ("b", 4, 1),
)
HITS_SENT, LOSS_DONE = 36, 78


def kernel(seqs, hidden_hbm, head_hbm, small, out, loss,
           hidden, head, in_sem,
           scores, peaks, grad, stats, hits,
           core_in, ya0, ya, za, yb0, yb, zb, last,
           lse_s, lse_r, hit_s, hit_r, core_s, core_r,
           ya_s, ya_r, za_s, za_r, yb_s, yb_r, zb_s, zb_r):
    vocab_rows, width = head.shape
    slots = hidden.shape[0]
    part = vocab_rows // NZ
    block = vocab_rows * width // LANES // (NZ * NY * NC)
    pitch = width // LANES
    rows_b = block - ROWS_A
    half_a, half_b = ROWS_A // 2, rows_b // 2

    depth = width // STEPS
    loads = []
    for i in range(STEPS):
        columns = pl.ds(i * depth, depth)
        loads.append((
            pltpu.make_async_copy(hidden_hbm.at[:, columns], hidden.at[:, columns], in_sem.at[0, i]),
            pltpu.make_async_copy(head_hbm.at[:, columns], head.at[:, columns], in_sem.at[1, i]),
        ))
        for load in loads[i]:
            load.start()

    v = lax.axis_index("vocab")
    d = lax.axis_index("dp")
    x = v % NX
    h = v // NX
    c = d % NC
    y = (d // NC) % NY
    z = d // (NC * NY)

    partner = d + 1 - 2 * c
    y_next = [(z * NY + (y + 1) % NY) * NC + c, (z * NY + (y + NY - 1) % NY) * NC + c]
    z_peer = [(((z + k) % NZ) * NY + y) * NC + c for k in (1, 2)]
    v_peers = [
        ((h + dh) % NH) * NX + (x + dx) % NX
        for dh in (2, 1, 3, 0) for dx in (2, 1, 3, 0) if dh or dx
    ]

    barrier = pltpu.get_barrier_semaphore()
    for peer in v_peers:
        pl.semaphore_signal(barrier, inc=1, device_id={"vocab": peer}, device_id_type=MESH)
    for peer in [partner] + y_next + z_peer:
        pl.semaphore_signal(barrier, inc=1, device_id={"dp": peer}, device_id_type=MESH)

    position = lax.broadcasted_iota(jnp.int32, (1, slots), 1)
    sizes = small[:, slots:slots + LANES]
    member, counts = [], []
    begin = jnp.zeros((1, 1), jnp.int32)
    weight = jnp.zeros((1, slots), F32)
    for k in range(seqs):
        count = sizes[:, k:k + 1]
        end = begin + count
        inside = (position >= begin) & (position < end)
        member.append(inside)
        counts.append(count.astype(F32))
        rate = sizes[:, seqs + k:seqs + k + 1].astype(F32) / counts[k]
        weight = jnp.where(inside, rate, weight)
        begin = end

    relative = small[:, 0:slots] - v * vocab_rows
    row = lax.broadcasted_iota(jnp.int32, (part, slots), 0)
    own_hit = jnp.zeros((1, slots), F32)
    part_lse = []
    for i in range(STEPS):
        for load in loads[i]:
            load.wait()
        columns = pl.ds(i * depth, depth)
        for k in range(NZ):
            value = lax.dot_general(
                head[pl.ds(k * part, part), columns], hidden[:, columns],
                (((1,), (1,)), ((), ())), preferred_element_type=F32,
            )
            if i > 0:
                value = value + scores[k]
            if i == STEPS - 1:
                peak = jnp.max(value, axis=0, keepdims=True)
                own_hit += jnp.sum(
                    jnp.where(row == relative - k * part, value, 0.0), axis=0, keepdims=True
                )
                value = jnp.exp(value - peak)
                peaks[k] = peak
                part_lse.append(peak + jnp.log(jnp.sum(value, axis=0, keepdims=True)))
            scores[k] = value

    def log_sum_exp(terms):
        top = terms[0]
        for term in terms[1:]:
            top = jnp.maximum(top, term)
        total = jnp.exp(terms[0] - top)
        for term in terms[1:]:
            total = total + jnp.exp(term - top)
        return top + jnp.log(total)

    stats[0] = log_sum_exp(part_lse)
    hits[0] = own_hit

    pl.semaphore_wait(barrier, NX * NH - 1 + 1 + 2 + 2)

    waits = []

    def send(src, dst, send_sem, recv_sem, axis, peer):
        copy = pltpu.make_async_remote_copy(
            src_ref=src, dst_ref=dst, send_sem=send_sem, recv_sem=recv_sem,
            device_id={axis: peer}, device_id_type=MESH,
        )
        copy.start()
        waits.append(copy)
        return copy

    def spread(ref, send_sem, recv_sem):
        return [
            send(ref.at[0], ref.at[s], send_sem.at[s], recv_sem.at[s], "vocab", peer)
            for s, peer in enumerate(v_peers, 1)
        ]

    def collect(copies, ref):
        for copy in copies:
            copy.wait_recv()
        return [ref[s] for s in range(NX * NH)]

    lse_copies = spread(stats, lse_s, lse_r)
    log_total = log_sum_exp(collect(lse_copies, stats))

    def line(zo, yo, co):
        return pl.multiple_of(((zo * NY + yo) * NC + co) * block, 8)

    def own(zo, yo, start, count):
        return pl.ds(pl.multiple_of(line(zo, yo, c) + start, 8), count)

    zone = [(z + 1) % NZ, (z + 2) % NZ, z]
    core_copies, ya_copies, za_copies, yb_copies, zb_copies = {}, {}, {}, {}, {}

    def product(k):
        zo = zone[k]
        onehot = jnp.where(row == relative - zo * part, 1.0, 0.0)
        shift = jnp.exp(peaks[zo] - log_total)
        rows = ((scores[zo] * shift - onehot) * weight).astype(jnp.bfloat16)
        value = jnp.dot(rows, hidden[...], preferred_element_type=F32)
        for j in range(pitch):
            grad[pl.ds(zo * part * pitch + j, part, stride=pitch), :] = value[:, j * LANES:(j + 1) * LANES]

    def swap(k, dist):
        i = DISTANCES.index(dist)
        core_copies[k, dist] = send(
            grad.at[pl.ds(line(zone[k], (y + dist) % NY, 1 - c), block)], core_in.at[k, i],
            core_s.at[k, i], core_r.at[k, i], "dp", partner,
        )

    def pair(k, dist):
        yo = (y + dist) % NY
        core_copies[k, dist].wait_recv()
        grad[own(zone[k], yo, 0, block), :] += core_in[k, DISTANCES.index(dist)]
        if dist == 4:
            for way in range(2):
                ya_copies[k, 0, way] = send(
                    grad.at[own(zone[k], yo, way * half_a, half_a)], ya0.at[k, way],
                    ya_s.at[k, 0, way], ya_r.at[k, 0, way], "dp", y_next[way],
                )
        if k < 2:
            zb_copies[k, dist] = send(
                grad.at[own(zone[k], yo, ROWS_A, rows_b)], zb.at[k, dist],
                zb_s.at[k, dist], zb_r.at[k, dist], "dp", z_peer[k],
            )

    def a(k, t, way):
        yo = (y + toward(way, t)) % NY
        ya_copies[k, t - 1, way].wait_recv()
        if t == 1:
            grad[own(zone[k], yo, way * half_a, half_a), :] += ya0[k, way]
        else:
            grad[own(zone[k], yo, 0, ROWS_A), :] += ya[k, t - 2, way]
        if t < 4:
            ya_copies[k, t, way] = send(
                grad.at[own(zone[k], yo, 0, ROWS_A)], ya.at[k, t - 1, way],
                ya_s.at[k, t, way], ya_r.at[k, t, way], "dp", y_next[way],
            )
            return
        closed.append((k, way))
        if k < 2 and (k, 1 - way) in closed:
            za_copies[k] = send(
                grad.at[own(zone[k], y, 0, ROWS_A)], za.at[k], za_s.at[k], za_r.at[k], "dp", z_peer[k]
            )

    closed = []

    def zsum(dist):
        yo = (y + dist) % NY
        for k in range(2):
            zb_copies[k, dist].wait_recv()
        grad[own(z, yo, ROWS_A, rows_b), :] += zb[0, dist] + zb[1, dist]
        if dist == 4:
            for way in range(2):
                yb_copies[0, way] = send(
                    grad.at[own(z, yo, ROWS_A + way * half_b, half_b)], yb0.at[way],
                    yb_s.at[0, way], yb_r.at[0, way], "dp", y_next[way],
                )

    def b(t, way):
        yo = (y + toward(way, t)) % NY
        yb_copies[t - 1, way].wait_recv()
        if t == 1:
            grad[own(z, yo, ROWS_A + way * half_b, half_b), :] += yb0[way]
        else:
            grad[own(z, yo, ROWS_A, rows_b), :] += yb[t - 2, way]
        if t < 4:
            yb_copies[t, way] = send(
                grad.at[own(z, yo, ROWS_A, rows_b)], yb.at[t - 1, way],
                yb_s.at[t, way], yb_r.at[t, way], "dp", y_next[way],
            )

    def end():
        for k in range(2):
            za_copies[k].wait_recv()
        last[pl.ds(0, ROWS_A), :] = grad[own(z, y, 0, ROWS_A), :] + za[0] + za[1]

    def finish_loss():
        target_logit = jnp.zeros((1, slots), F32)
        for term in collect(hit_copies, hits):
            target_logit = target_logit + term
        cross = log_total - target_logit
        for k in range(seqs):
            mean = jnp.where(member[k], cross, 0.0) / counts[k]
            loss[k] = jnp.sum(mean)

    steps = {"product": product, "swap": swap, "pair": pair, "a": a, "zsum": zsum, "b": b, "end": end}
    for number, (kind, *where) in enumerate(ORDER):
        if number == HITS_SENT:
            hit_copies = spread(hits, hit_s, hit_r)
        if number == LOSS_DONE:
            finish_loss()
        steps[kind](*where)

    last[pl.ds(ROWS_A, rows_b), :] = grad[own(z, y, ROWS_A, rows_b), :]
    for j in range(pitch):
        out[:, j * LANES:(j + 1) * LANES] = last[pl.ds(j, out.shape[0], stride=pitch), :]

    for copy in waits:
        copy.wait_send()


def on_device(hidden, head, targets, mask_counts, answer_lengths):
    vocab_rows, width = head.shape
    slots = hidden.shape[0]
    lines = vocab_rows * width // LANES
    block = lines // (NZ * NY * NC)
    rows_b = block - ROWS_A
    anywhere = pl.BlockSpec(memory_space=pl.ANY)
    vmem = pl.BlockSpec(memory_space=pltpu.VMEM)
    smem = pl.BlockSpec(memory_space=pltpu.SMEM)
    dma = pltpu.SemaphoreType.DMA
    seqs = mask_counts.shape[0]
    small = jnp.concatenate(
        [targets, mask_counts, answer_lengths, jnp.zeros((LANES - 2 * seqs,), jnp.int32)]
    ).reshape(1, slots + LANES)
    head_grad, seq_loss = pl.pallas_call(
        functools.partial(kernel, seqs),
        out_shape=(
            jax.ShapeDtypeStruct((vocab_rows // (NZ * NY * NC), width), F32),
            jax.ShapeDtypeStruct(mask_counts.shape, F32),
        ),
        in_specs=[anywhere, anywhere, vmem],
        out_specs=(vmem, smem),
        scratch_shapes=[
            pltpu.VMEM(hidden.shape, hidden.dtype),
            pltpu.VMEM(head.shape, head.dtype),
            dma((2, STEPS)),
            pltpu.VMEM((NZ, vocab_rows // NZ, slots), F32),
            pltpu.VMEM((NZ, 1, slots), F32),
            pltpu.VMEM((lines, LANES), F32),
            pltpu.VMEM((NX * NH, 1, slots), F32),
            pltpu.VMEM((NX * NH, 1, slots), F32),
            pltpu.VMEM((NZ, NY, block, LANES), F32),
            pltpu.VMEM((NZ, 2, ROWS_A // 2, LANES), F32),
            pltpu.VMEM((NZ, 3, 2, ROWS_A, LANES), F32),
            pltpu.VMEM((2, ROWS_A, LANES), F32),
            pltpu.VMEM((2, rows_b // 2, LANES), F32),
            pltpu.VMEM((3, 2, rows_b, LANES), F32),
            pltpu.VMEM((2, NY, rows_b, LANES), F32),
            pltpu.VMEM((block, LANES), F32),
            dma((NX * NH,)), dma((NX * NH,)),
            dma((NX * NH,)), dma((NX * NH,)),
            dma((NZ, NY)), dma((NZ, NY)),
            dma((NZ, 4, 2)), dma((NZ, 4, 2)),
            dma((2,)), dma((2,)),
            dma((4, 2)), dma((4, 2)),
            dma((2, NY)), dma((2, NY)),
        ],
        compiler_params=pltpu.CompilerParams(
            collective_id=0, has_side_effects=True, vmem_limit_bytes=52 * 1024 * 1024
        ),
        cost_estimate=pl.CostEstimate(
            flops=4 * vocab_rows * slots * width,
            bytes_accessed=2 * (vocab_rows + slots) * width,
            transcendentals=vocab_rows * slots,
        ),
        name="head_gradient",
    )(hidden, head, small)
    return seq_loss, head_grad


def solution(mesh):
    return jax.shard_map(
        on_device,
        mesh=mesh,
        in_specs=(P("dp", None), P("vocab", None), P("dp"), P("dp"), P("dp")),
        out_specs=(P("dp"), P(("vocab", "dp"), None)),
        check_vma=False,
    )
```

```python
import functools

import jax
import jax.numpy as jnp
from jax import lax
from jax.experimental import pallas as pl
from jax.experimental.pallas import tpu as pltpu
from jax.sharding import PartitionSpec as P

MESH = pl.DeviceIdType.MESH
F32 = jnp.float32

NX, NH = 4, 4
NZ, NY, NC = 3, 8, 2
LANES = 128
STEPS = 4
ROWS_A = 176
HALVES_A, HALVES_B = (88, 88), (56, 56)
DISTANCES = (4, 3, 5, 2, 6, 1, 7, 0)


def toward(way, t):
    return (4 - t if way == 0 else 4 + t) % NY


ORDER = (
    ("product", 1, 0), ("swap", 1, 4), ("product", 0, 0), ("swap", 0, 4), ("pair", 1, 4), ("product", 2, 0),
    ("swap", 2, 4), ("pair", 0, 4), ("product", 1, 1), ("swap", 1, 3), ("swap", 1, 5), ("pair", 2, 4),
    ("product", 0, 1), ("swap", 0, 7), ("swap", 0, 3), ("pair", 1, 3), ("swap", 0, 5), ("swap", 1, 6), ("pair", 1, 5),
    ("a", 1, 1, 0), ("a", 1, 1, 1), ("product", 2, 1), ("pair", 0, 3), ("swap", 1, 2), ("zsum", 4), ("a", 0, 1, 0),
    ("pair", 1, 6), ("swap", 0, 0), ("pair", 0, 5), ("a", 0, 1, 1), ("swap", 2, 3), ("swap", 2, 5), ("swap", 2, 0),
    ("swap", 0, 2), ("swap", 2, 6), ("pair", 2, 3), ("pair", 1, 2), ("pair", 2, 5), ("swap", 0, 6), ("swap", 1, 7),
    ("a", 2, 1, 0), ("a", 2, 1, 1), ("pair", 0, 2), ("swap", 2, 2), ("swap", 1, 1), ("pair", 0, 6), ("a", 1, 2, 0),
    ("pair", 2, 2), ("a", 1, 2, 1), ("swap", 1, 0), ("pair", 2, 6), ("pair", 1, 7), ("a", 0, 2, 0), ("swap", 2, 1),
    ("a", 0, 2, 1), ("a", 2, 2, 1), ("zsum", 3), ("pair", 0, 0), ("b", 1, 0), ("swap", 0, 1), ("zsum", 2),
    ("zsum", 5), ("pair", 1, 0), ("pair", 1, 1), ("a", 1, 3, 0), ("b", 1, 1), ("pair", 0, 1), ("a", 2, 2, 0),
    ("a", 1, 3, 1), ("pair", 0, 7), ("zsum", 6), ("a", 0, 3, 1), ("swap", 2, 7), ("a", 0, 3, 0), ("pair", 2, 1),
    ("hits",), ("pair", 2, 7), ("b", 2, 0), ("pair", 2, 0), ("b", 2, 1), ("a", 2, 3, 1), ("a", 2, 3, 0),
    ("a", 1, 4, 1), ("a", 1, 4, 0), ("zsum", 7), ("a", 0, 4, 0), ("zsum", 1), ("zsum", 0), ("a", 0, 4, 1),
    ("b", 3, 0), ("b", 3, 1), ("a", 2, 4, 0), ("loss",), ("a", 2, 4, 1), ("sent",), ("end",), ("b", 4, 0),
    ("b", 4, 1),
)


def kernel(seqs, hidden_hbm, head_hbm, small, out, loss,
           hidden, head, in_sem,
           scores, marks, peaks, grad, stats, hits,
           core_in, ya0, ya, za, yb0, yb, zb, last,
           lse_s, lse_r, hit_s, hit_r, core_s, core_r,
           ya_s, ya_r, za_s, za_r, yb_s, yb_r, zb_s, zb_r):
    vocab_rows, width = head.shape
    slots = hidden.shape[0]
    part = vocab_rows // NZ
    block = vocab_rows * width // LANES // (NZ * NY * NC)
    pitch = width // LANES
    rows_b = block - ROWS_A
    from_a, from_b = (0, HALVES_A[0]), (ROWS_A, ROWS_A + HALVES_B[0])

    depth = width // STEPS
    loads = []
    for i in range(STEPS):
        columns = pl.ds(i * depth, depth)
        loads.append((
            pltpu.make_async_copy(hidden_hbm.at[:, columns], hidden.at[:, columns], in_sem.at[0, i]),
            pltpu.make_async_copy(head_hbm.at[:, columns], head.at[:, columns], in_sem.at[1, i]),
        ))
        for load in loads[i]:
            load.start()

    v = lax.axis_index("vocab")
    d = lax.axis_index("dp")
    x = v % NX
    h = v // NX
    c = d % NC
    y = (d // NC) % NY
    z = d // (NC * NY)

    partner = d + 1 - 2 * c
    y_next = [(z * NY + (y + 1) % NY) * NC + c, (z * NY + (y + NY - 1) % NY) * NC + c]
    z_peer = [(((z + k) % NZ) * NY + y) * NC + c for k in (1, 2)]
    v_peers = [
        ((h + dh) % NH) * NX + (x + dx) % NX
        for dh in (2, 1, 3, 0) for dx in (2, 1, 3, 0) if dh or dx
    ]

    barrier = pltpu.get_barrier_semaphore()
    for peer in v_peers:
        pl.semaphore_signal(barrier, inc=1, device_id={"vocab": peer}, device_id_type=MESH)
    for peer in [partner] + y_next + z_peer:
        pl.semaphore_signal(barrier, inc=1, device_id={"dp": peer}, device_id_type=MESH)

    position = lax.broadcasted_iota(jnp.int32, (1, slots), 1)
    sizes = small[:, slots:slots + LANES]
    member, counts = [], []
    begin = jnp.zeros((1, 1), jnp.int32)
    weight = jnp.zeros((1, slots), F32)
    for k in range(seqs):
        count = sizes[:, k:k + 1]
        end = begin + count
        inside = (position >= begin) & (position < end)
        member.append(inside)
        counts.append(count.astype(F32))
        rate = sizes[:, seqs + k:seqs + k + 1].astype(F32) / counts[k]
        weight = jnp.where(inside, rate, weight)
        begin = end

    relative = small[:, 0:slots] - v * vocab_rows
    row = lax.broadcasted_iota(jnp.int32, (part, slots), 0)
    part_lse = []
    for i in range(STEPS):
        for load in loads[i]:
            load.wait()
        columns = pl.ds(i * depth, depth)
        for k in range(NZ):
            value = lax.dot_general(
                head[pl.ds(k * part, part), columns], hidden[:, columns],
                (((1,), (1,)), ((), ())), preferred_element_type=F32,
            )
            if i > 0:
                value = value + scores[k]
            if i == STEPS - 1:
                peak = jnp.max(value, axis=0, keepdims=True)
                marks[k] = value
                value = jnp.exp(value - peak)
                peaks[k] = peak
                part_lse.append(peak + jnp.log(jnp.sum(value, axis=0, keepdims=True)))
            scores[k] = value

    def log_sum_exp(terms):
        top = terms[0]
        for term in terms[1:]:
            top = jnp.maximum(top, term)
        total = jnp.exp(terms[0] - top)
        for term in terms[1:]:
            total = total + jnp.exp(term - top)
        return top + jnp.log(total)

    stats[0] = log_sum_exp(part_lse)

    pl.semaphore_wait(barrier, NX * NH - 1 + 1 + 2 + 2)

    waits = []

    def send(src, dst, send_sem, recv_sem, axis, peer):
        copy = pltpu.make_async_remote_copy(
            src_ref=src, dst_ref=dst, send_sem=send_sem, recv_sem=recv_sem,
            device_id={axis: peer}, device_id_type=MESH,
        )
        copy.start()
        waits.append(copy)
        return copy

    def spread(ref, send_sem, recv_sem):
        return [
            send(ref.at[0], ref.at[s], send_sem.at[s], recv_sem.at[s], "vocab", peer)
            for s, peer in enumerate(v_peers, 1)
        ]

    def collect(copies, ref):
        for copy in copies:
            copy.wait_recv()
        return [ref[s] for s in range(NX * NH)]

    lse_copies = spread(stats, lse_s, lse_r)

    own_hit = jnp.zeros((1, slots), F32)
    for k in range(NZ):
        hit = row == relative - k * part
        own_hit += jnp.sum(jnp.where(hit, marks[k], 0.0), axis=0, keepdims=True)
        marks[k] = jnp.where(hit, weight, 0.0)
    hits[0] = own_hit

    log_total = log_sum_exp(collect(lse_copies, stats))

    def line(zo, yo, co):
        return pl.multiple_of(((zo * NY + yo) * NC + co) * block, 8)

    def own(zo, yo, start, count):
        return pl.ds(pl.multiple_of(line(zo, yo, c) + start, 8), count)

    zone = [(z + 1) % NZ, (z + 2) % NZ, z]
    core_copies, ya_copies, za_copies, yb_copies, zb_copies = {}, {}, {}, {}, {}

    def product(k, second):
        zo = zone[k]
        half = part // 2
        start = pl.multiple_of((((y + 4) % NY) // 4 + second) % 2 * half, 8)
        rows = pl.ds(start, half)
        scale = jnp.exp(peaks[zo] - log_total) * weight
        value = (scores[zo, rows, :] * scale - marks[zo, rows, :]).astype(jnp.bfloat16)
        value = jnp.dot(value, hidden[...], preferred_element_type=F32)
        first = (zo * part + start) * pitch
        for j in range(pitch):
            grad[pl.ds(first + j, half, stride=pitch), :] = value[:, j * LANES:(j + 1) * LANES]

    def swap(k, dist):
        i = DISTANCES.index(dist)
        core_copies[k, dist] = send(
            grad.at[pl.ds(line(zone[k], (y + dist) % NY, 1 - c), block)], core_in.at[k, i],
            core_s.at[k, i], core_r.at[k, i], "dp", partner,
        )

    def pair(k, dist):
        yo = (y + dist) % NY
        core_copies[k, dist].wait_recv()
        grad[own(zone[k], yo, 0, block), :] += core_in[k, DISTANCES.index(dist)]
        if dist == 4:
            for way in range(2):
                ya_copies[k, 0, way] = send(
                    grad.at[own(zone[k], yo, from_a[way], HALVES_A[way])],
                    ya0.at[k, way, pl.ds(0, HALVES_A[way])],
                    ya_s.at[k, 0, way], ya_r.at[k, 0, way], "dp", y_next[way],
                )
        if k < 2:
            zb_copies[k, dist] = send(
                grad.at[own(zone[k], yo, ROWS_A, rows_b)], zb.at[k, dist],
                zb_s.at[k, dist], zb_r.at[k, dist], "dp", z_peer[k],
            )

    def a(k, t, way):
        yo = (y + toward(way, t)) % NY
        ya_copies[k, t - 1, way].wait_recv()
        if t == 1:
            grad[own(zone[k], yo, from_a[way], HALVES_A[way]), :] += ya0[k, way, pl.ds(0, HALVES_A[way]), :]
        else:
            grad[own(zone[k], yo, 0, ROWS_A), :] += ya[k, t - 2, way]
        if t < 4:
            ya_copies[k, t, way] = send(
                grad.at[own(zone[k], yo, 0, ROWS_A)], ya.at[k, t - 1, way],
                ya_s.at[k, t, way], ya_r.at[k, t, way], "dp", y_next[way],
            )
            return
        closed.append((k, way))
        if k < 2 and (k, 1 - way) in closed:
            za_copies[k] = send(
                grad.at[own(zone[k], y, 0, ROWS_A)], za.at[k], za_s.at[k], za_r.at[k], "dp", z_peer[k]
            )

    closed = []

    def zsum(dist):
        yo = (y + dist) % NY
        for k in range(2):
            zb_copies[k, dist].wait_recv()
        grad[own(z, yo, ROWS_A, rows_b), :] += zb[0, dist] + zb[1, dist]
        if dist == 4:
            for way in range(2):
                yb_copies[0, way] = send(
                    grad.at[own(z, yo, from_b[way], HALVES_B[way])],
                    yb0.at[way, pl.ds(0, HALVES_B[way])],
                    yb_s.at[0, way], yb_r.at[0, way], "dp", y_next[way],
                )

    def b(t, way):
        yo = (y + toward(way, t)) % NY
        yb_copies[t - 1, way].wait_recv()
        if t == 1:
            grad[own(z, yo, from_b[way], HALVES_B[way]), :] += yb0[way, pl.ds(0, HALVES_B[way]), :]
        else:
            grad[own(z, yo, ROWS_A, rows_b), :] += yb[t - 2, way]
        if t < 4:
            yb_copies[t, way] = send(
                grad.at[own(z, yo, ROWS_A, rows_b)], yb.at[t - 1, way],
                yb_s.at[t, way], yb_r.at[t, way], "dp", y_next[way],
            )

    def end():
        for k in range(2):
            za_copies[k].wait_recv()
        last[pl.ds(0, ROWS_A), :] = grad[own(z, y, 0, ROWS_A), :] + za[0] + za[1]

    hit_copies = []

    def send_hits():
        hit_copies.extend(spread(hits, hit_s, hit_r))

    def finish_loss():
        target_logit = jnp.zeros((1, slots), F32)
        for term in collect(hit_copies, hits):
            target_logit = target_logit + term
        cross = log_total - target_logit
        for k in range(seqs):
            mean = jnp.where(member[k], cross, 0.0) / counts[k]
            loss[k] = jnp.sum(mean)

    def sent():
        for copy in waits[:-16]:
            copy.wait_send()
        del waits[:-16]

    steps = {"product": product, "swap": swap, "pair": pair, "a": a, "zsum": zsum, "b": b, "end": end,
             "hits": send_hits, "loss": finish_loss, "sent": sent}
    for kind, *where in ORDER:
        steps[kind](*where)

    last[pl.ds(ROWS_A, rows_b), :] = grad[own(z, y, ROWS_A, rows_b), :]
    for j in range(pitch):
        out[:, j * LANES:(j + 1) * LANES] = last[pl.ds(j, out.shape[0], stride=pitch), :]

    for copy in waits:
        copy.wait_send()


def on_device(hidden, head, targets, mask_counts, answer_lengths):
    vocab_rows, width = head.shape
    slots = hidden.shape[0]
    lines = vocab_rows * width // LANES
    block = lines // (NZ * NY * NC)
    rows_b = block - ROWS_A
    anywhere = pl.BlockSpec(memory_space=pl.ANY)
    vmem = pl.BlockSpec(memory_space=pltpu.VMEM)
    smem = pl.BlockSpec(memory_space=pltpu.SMEM)
    dma = pltpu.SemaphoreType.DMA
    seqs = mask_counts.shape[0]
    small = jnp.concatenate(
        [targets, mask_counts, answer_lengths, jnp.zeros((LANES - 2 * seqs,), jnp.int32)]
    ).reshape(1, slots + LANES)
    head_grad, seq_loss = pl.pallas_call(
        functools.partial(kernel, seqs),
        out_shape=(
            jax.ShapeDtypeStruct((vocab_rows // (NZ * NY * NC), width), F32),
            jax.ShapeDtypeStruct(mask_counts.shape, F32),
        ),
        in_specs=[anywhere, anywhere, vmem],
        out_specs=(vmem, smem),
        scratch_shapes=[
            pltpu.VMEM(hidden.shape, hidden.dtype),
            pltpu.VMEM(head.shape, head.dtype),
            dma((2, STEPS)),
            pltpu.VMEM((NZ, vocab_rows // NZ, slots), F32),
            pltpu.VMEM((NZ, vocab_rows // NZ, slots), F32),
            pltpu.VMEM((NZ, 1, slots), F32),
            pltpu.VMEM((lines, LANES), F32),
            pltpu.VMEM((NX * NH, 1, slots), F32),
            pltpu.VMEM((NX * NH, 1, slots), F32),
            pltpu.VMEM((NZ, NY, block, LANES), F32),
            pltpu.VMEM((NZ, 2, max(HALVES_A), LANES), F32),
            pltpu.VMEM((NZ, 3, 2, ROWS_A, LANES), F32),
            pltpu.VMEM((2, ROWS_A, LANES), F32),
            pltpu.VMEM((2, max(HALVES_B), LANES), F32),
            pltpu.VMEM((3, 2, rows_b, LANES), F32),
            pltpu.VMEM((2, NY, rows_b, LANES), F32),
            pltpu.VMEM((block, LANES), F32),
            dma((NX * NH,)), dma((NX * NH,)),
            dma((NX * NH,)), dma((NX * NH,)),
            dma((NZ, NY)), dma((NZ, NY)),
            dma((NZ, 4, 2)), dma((NZ, 4, 2)),
            dma((2,)), dma((2,)),
            dma((4, 2)), dma((4, 2)),
            dma((2, NY)), dma((2, NY)),
        ],
        compiler_params=pltpu.CompilerParams(
            collective_id=0, has_side_effects=True, vmem_limit_bytes=52 * 1024 * 1024
        ),
        cost_estimate=pl.CostEstimate(
            flops=4 * vocab_rows * slots * width,
            bytes_accessed=2 * (vocab_rows + slots) * width,
            transcendentals=vocab_rows * slots,
        ),
        name="head_gradient",
    )(hidden, head, small)
    return seq_loss, head_grad


def solution(mesh):
    return jax.shard_map(
        on_device,
        mesh=mesh,
        in_specs=(P("dp", None), P("vocab", None), P("dp"), P("dp"), P("dp")),
        out_specs=(P("dp"), P(("vocab", "dp"), None)),
        check_vma=False,
    )
```

```python
import jax
import jax.numpy as jnp
from jax import lax
from jax.experimental import pallas as pl
from jax.experimental.pallas import tpu as pltpu
from jax.sharding import PartitionSpec as P

MESH = pl.DeviceIdType.MESH
F32 = jnp.float32

NX, NH = 4, 4
NZ, NY, NC = 3, 8, 2
LANES = 128
STEPS = 4
ROWS_A = 176
HALVES_A, HALVES_B = (88, 88), (56, 56)
DISTANCES = (4, 3, 5, 2, 6, 1, 7, 0)


def toward(way, t):
    return (4 - t if way == 0 else 4 + t) % NY


ORDER = (
    ("product", 1, 0), ("swap", 1, 4), ("product", 0, 0), ("swap", 0, 4), ("pair", 1, 4), ("product", 2, 0),
    ("swap", 2, 4), ("pair", 0, 4), ("product", 1, 1), ("swap", 1, 3), ("swap", 1, 5), ("pair", 2, 4),
    ("product", 0, 1), ("swap", 0, 7), ("swap", 0, 3), ("pair", 1, 3), ("swap", 0, 5), ("swap", 1, 6), ("pair", 1, 5),
    ("a", 1, 1, 0), ("a", 1, 1, 1), ("product", 2, 1), ("pair", 0, 3), ("swap", 1, 2), ("zsum", 4), ("a", 0, 1, 0),
    ("pair", 1, 6), ("swap", 0, 0), ("pair", 0, 5), ("a", 0, 1, 1), ("swap", 2, 3), ("swap", 2, 5), ("swap", 2, 0),
    ("swap", 0, 2), ("swap", 2, 6), ("pair", 2, 3), ("pair", 1, 2), ("pair", 2, 5), ("swap", 0, 6), ("swap", 1, 7),
    ("a", 2, 1, 0), ("a", 2, 1, 1), ("pair", 0, 2), ("swap", 2, 2), ("swap", 1, 1), ("pair", 0, 6), ("a", 1, 2, 0),
    ("pair", 2, 2), ("a", 1, 2, 1), ("swap", 1, 0), ("pair", 2, 6), ("pair", 1, 7), ("a", 0, 2, 0), ("swap", 2, 1),
    ("a", 0, 2, 1), ("a", 2, 2, 1), ("zsum", 3), ("pair", 0, 0), ("b", 1, 0), ("swap", 0, 1), ("zsum", 2),
    ("zsum", 5), ("pair", 1, 0), ("pair", 1, 1), ("a", 1, 3, 0), ("b", 1, 1), ("pair", 0, 1), ("a", 2, 2, 0),
    ("a", 1, 3, 1), ("pair", 0, 7), ("zsum", 6), ("a", 0, 3, 1), ("swap", 2, 7), ("a", 0, 3, 0), ("pair", 2, 1),
    ("hits",), ("pair", 2, 7), ("b", 2, 0), ("pair", 2, 0), ("b", 2, 1), ("a", 2, 3, 1), ("a", 2, 3, 0),
    ("a", 1, 4, 1), ("a", 1, 4, 0), ("zsum", 7), ("a", 0, 4, 0), ("zsum", 1), ("zsum", 0), ("a", 0, 4, 1),
    ("b", 3, 0), ("b", 3, 1), ("a", 2, 4, 0), ("loss",), ("a", 2, 4, 1), ("sent",), ("end",), ("b", 4, 0),
    ("b", 4, 1),
)


def kernel(hidden_hbm, head_hbm, targets_hbm, counts_hbm, lengths_hbm, out, loss,
           hidden, head, targets, counts, lengths, in_sem, small_sem,
           scores, marks, peaks, grad, stats, hits,
           core_in, ya0, ya, za, yb0, yb, zb, last,
           lse_s, lse_r, hit_s, hit_r, core_s, core_r,
           ya_s, ya_r, za_s, za_r, yb_s, yb_r, zb_s, zb_r):
    vocab_rows, width = head.shape
    slots = hidden.shape[0]
    part = vocab_rows // NZ
    block = vocab_rows * width // LANES // (NZ * NY * NC)
    pitch = width // LANES
    rows_b = block - ROWS_A
    from_a, from_b = (0, HALVES_A[0]), (ROWS_A, ROWS_A + HALVES_B[0])

    v = lax.axis_index("vocab")
    d = lax.axis_index("dp")
    x = v % NX
    h = v // NX
    c = d % NC
    y = (d // NC) % NY
    z = d // (NC * NY)

    partner = d + 1 - 2 * c
    y_next = [(z * NY + (y + 1) % NY) * NC + c, (z * NY + (y + NY - 1) % NY) * NC + c]
    z_peer = [(((z + k) % NZ) * NY + y) * NC + c for k in (1, 2)]
    v_peers = [
        ((h + dh) % NH) * NX + (x + dx) % NX
        for dh in (2, 1, 3, 0) for dx in (2, 1, 3, 0) if dh or dx
    ]

    barrier = pltpu.get_barrier_semaphore()
    for peer in v_peers:
        pl.semaphore_signal(barrier, inc=1, device_id={"vocab": peer}, device_id_type=MESH)
    seqs = counts.shape[0]
    depth = width // STEPS
    loads = []
    for i in range(STEPS):
        columns = pl.ds(i * depth, depth)
        loads.append((
            pltpu.make_async_copy(hidden_hbm.at[:, columns], hidden.at[:, columns], in_sem.at[0, i]),
            pltpu.make_async_copy(head_hbm.at[:, columns], head.at[:, columns], in_sem.at[1, i]),
        ))
        for load in loads[i]:
            load.start()
    small_loads = [
        pltpu.make_async_copy(targets_hbm, targets, small_sem.at[0]),
        pltpu.make_async_copy(counts_hbm, counts, small_sem.at[1]),
        pltpu.make_async_copy(lengths_hbm, lengths, small_sem.at[2]),
    ]
    for load in small_loads:
        load.start()
    for peer in [partner] + y_next + z_peer:
        pl.semaphore_signal(barrier, inc=1, device_id={"dp": peer}, device_id_type=MESH)

    row = lax.broadcasted_iota(jnp.int32, (part, slots), 0)
    part_lse = []
    for i in range(STEPS):
        for load in loads[i]:
            load.wait()
        columns = pl.ds(i * depth, depth)
        for k in range(NZ):
            value = lax.dot_general(
                head[pl.ds(k * part, part), columns], hidden[:, columns],
                (((1,), (1,)), ((), ())), preferred_element_type=F32,
            )
            if i > 0:
                value = value + scores[k]
            if i == STEPS - 1:
                peak = jnp.max(value, axis=0, keepdims=True)
                marks[k] = value
                value = jnp.exp(value - peak)
                peaks[k] = peak
                part_lse.append(peak + jnp.log(jnp.sum(value, axis=0, keepdims=True)))
            scores[k] = value

    def log_sum_exp(terms):
        top = terms[0]
        for term in terms[1:]:
            top = jnp.maximum(top, term)
        total = jnp.exp(terms[0] - top)
        for term in terms[1:]:
            total = total + jnp.exp(term - top)
        return top + jnp.log(total)

    stats[0] = log_sum_exp(part_lse)

    pl.semaphore_wait(barrier, NX * NH - 1 + 1 + 2 + 2)

    waits = []

    def send(src, dst, send_sem, recv_sem, axis, peer):
        copy = pltpu.make_async_remote_copy(
            src_ref=src, dst_ref=dst, send_sem=send_sem, recv_sem=recv_sem,
            device_id={axis: peer}, device_id_type=MESH,
        )
        copy.start()
        waits.append(copy)
        return copy

    def spread(ref, send_sem, recv_sem):
        return [
            send(ref.at[0], ref.at[s], send_sem.at[s], recv_sem.at[s], "vocab", peer)
            for s, peer in enumerate(v_peers, 1)
        ]

    def collect(copies, ref):
        for copy in copies:
            copy.wait_recv()
        return [ref[s] for s in range(NX * NH)]

    lse_copies = spread(stats, lse_s, lse_r)

    for load in small_loads:
        load.wait()
    position = lax.broadcasted_iota(jnp.int32, (1, slots), 1)
    member, sizes = [], []
    begin = jnp.int32(0)
    weight = jnp.zeros((1, slots), F32)
    for k in range(seqs):
        end_of = begin + counts[k]
        inside = (position >= begin) & (position < end_of)
        member.append(inside)
        sizes.append(jnp.full((1, slots), counts[k], jnp.int32).astype(F32))
        rate = jnp.full((1, slots), lengths[k], jnp.int32).astype(F32) / sizes[k]
        weight = jnp.where(inside, rate, weight)
        begin = end_of

    relative = targets[...].reshape(1, slots) - v * vocab_rows
    own_hit = jnp.zeros((1, slots), F32)
    for k in range(NZ):
        hit = row == relative - k * part
        own_hit += jnp.sum(jnp.where(hit, marks[k], 0.0), axis=0, keepdims=True)
        marks[k] = jnp.where(hit, weight, 0.0)
    hits[0] = own_hit

    log_total = log_sum_exp(collect(lse_copies, stats))

    def line(zo, yo, co):
        return pl.multiple_of(((zo * NY + yo) * NC + co) * block, 8)

    def own(zo, yo, start, count):
        return pl.ds(pl.multiple_of(line(zo, yo, c) + start, 8), count)

    zone = [(z + 1) % NZ, (z + 2) % NZ, z]
    core_copies, ya_copies, za_copies, yb_copies, zb_copies = {}, {}, {}, {}, {}

    def product(k, second):
        zo = zone[k]
        half = part // 2
        start = pl.multiple_of((((y + 4) % NY) // 4 + second) % 2 * half, 8)
        rows = pl.ds(start, half)
        scale = jnp.exp(peaks[zo] - log_total) * weight
        value = (scores[zo, rows, :] * scale - marks[zo, rows, :]).astype(jnp.bfloat16)
        value = jnp.dot(value, hidden[...], preferred_element_type=F32)
        first = (zo * part + start) * pitch
        for j in range(pitch):
            grad[pl.ds(first + j, half, stride=pitch), :] = value[:, j * LANES:(j + 1) * LANES]

    def swap(k, dist):
        i = DISTANCES.index(dist)
        core_copies[k, dist] = send(
            grad.at[pl.ds(line(zone[k], (y + dist) % NY, 1 - c), block)], core_in.at[k, i],
            core_s.at[k, i], core_r.at[k, i], "dp", partner,
        )

    def pair(k, dist):
        yo = (y + dist) % NY
        core_copies[k, dist].wait_recv()
        grad[own(zone[k], yo, 0, block), :] += core_in[k, DISTANCES.index(dist)]
        if dist == 4:
            for way in range(2):
                ya_copies[k, 0, way] = send(
                    grad.at[own(zone[k], yo, from_a[way], HALVES_A[way])],
                    ya0.at[k, way, pl.ds(0, HALVES_A[way])],
                    ya_s.at[k, 0, way], ya_r.at[k, 0, way], "dp", y_next[way],
                )
        if k < 2:
            zb_copies[k, dist] = send(
                grad.at[own(zone[k], yo, ROWS_A, rows_b)], zb.at[k, dist],
                zb_s.at[k, dist], zb_r.at[k, dist], "dp", z_peer[k],
            )

    def a(k, t, way):
        yo = (y + toward(way, t)) % NY
        ya_copies[k, t - 1, way].wait_recv()
        if t == 1:
            grad[own(zone[k], yo, from_a[way], HALVES_A[way]), :] += ya0[k, way, pl.ds(0, HALVES_A[way]), :]
        else:
            grad[own(zone[k], yo, 0, ROWS_A), :] += ya[k, t - 2, way]
        if t < 4:
            ya_copies[k, t, way] = send(
                grad.at[own(zone[k], yo, 0, ROWS_A)], ya.at[k, t - 1, way],
                ya_s.at[k, t, way], ya_r.at[k, t, way], "dp", y_next[way],
            )
            return
        closed.append((k, way))
        if k < 2 and (k, 1 - way) in closed:
            za_copies[k] = send(
                grad.at[own(zone[k], y, 0, ROWS_A)], za.at[k], za_s.at[k], za_r.at[k], "dp", z_peer[k]
            )

    closed = []

    def zsum(dist):
        yo = (y + dist) % NY
        for k in range(2):
            zb_copies[k, dist].wait_recv()
        grad[own(z, yo, ROWS_A, rows_b), :] += zb[0, dist] + zb[1, dist]
        if dist == 4:
            for way in range(2):
                yb_copies[0, way] = send(
                    grad.at[own(z, yo, from_b[way], HALVES_B[way])],
                    yb0.at[way, pl.ds(0, HALVES_B[way])],
                    yb_s.at[0, way], yb_r.at[0, way], "dp", y_next[way],
                )

    def b(t, way):
        yo = (y + toward(way, t)) % NY
        yb_copies[t - 1, way].wait_recv()
        if t == 1:
            grad[own(z, yo, from_b[way], HALVES_B[way]), :] += yb0[way, pl.ds(0, HALVES_B[way]), :]
        else:
            grad[own(z, yo, ROWS_A, rows_b), :] += yb[t - 2, way]
        if t < 4:
            yb_copies[t, way] = send(
                grad.at[own(z, yo, ROWS_A, rows_b)], yb.at[t - 1, way],
                yb_s.at[t, way], yb_r.at[t, way], "dp", y_next[way],
            )

    def end():
        for k in range(2):
            za_copies[k].wait_recv()
        last[pl.ds(0, ROWS_A), :] = grad[own(z, y, 0, ROWS_A), :] + za[0] + za[1]

    hit_copies = []

    def send_hits():
        hit_copies.extend(spread(hits, hit_s, hit_r))

    def finish_loss():
        target_logit = jnp.zeros((1, slots), F32)
        for term in collect(hit_copies, hits):
            target_logit = target_logit + term
        cross = log_total - target_logit
        for k in range(seqs):
            mean = jnp.where(member[k], cross, 0.0) / sizes[k]
            loss[k] = jnp.sum(mean)

    def sent():
        for copy in waits[:-16]:
            copy.wait_send()
        del waits[:-16]

    steps = {"product": product, "swap": swap, "pair": pair, "a": a, "zsum": zsum, "b": b, "end": end,
             "hits": send_hits, "loss": finish_loss, "sent": sent}
    for kind, *where in ORDER:
        steps[kind](*where)

    last[pl.ds(ROWS_A, rows_b), :] = grad[own(z, y, ROWS_A, rows_b), :]
    for j in range(pitch):
        out[:, j * LANES:(j + 1) * LANES] = last[pl.ds(j, out.shape[0], stride=pitch), :]

    for copy in waits:
        copy.wait_send()


def on_device(hidden, head, targets, mask_counts, answer_lengths):
    vocab_rows, width = head.shape
    slots = hidden.shape[0]
    lines = vocab_rows * width // LANES
    block = lines // (NZ * NY * NC)
    rows_b = block - ROWS_A
    anywhere = pl.BlockSpec(memory_space=pltpu.HBM)
    vmem = pl.BlockSpec(memory_space=pltpu.VMEM)
    smem = pl.BlockSpec(memory_space=pltpu.SMEM)
    dma = pltpu.SemaphoreType.DMA
    arguments = [
        pltpu.with_memory_space_constraint(argument, pltpu.HBM)
        for argument in (hidden, head, targets, mask_counts, answer_lengths)
    ]
    head_grad, seq_loss = pl.pallas_call(
        kernel,
        out_shape=(
            jax.ShapeDtypeStruct((vocab_rows // (NZ * NY * NC), width), F32),
            jax.ShapeDtypeStruct(mask_counts.shape, F32),
        ),
        in_specs=[anywhere] * 5,
        out_specs=(vmem, smem),
        scratch_shapes=[
            pltpu.VMEM(hidden.shape, hidden.dtype),
            pltpu.VMEM(head.shape, head.dtype),
            pltpu.VMEM(targets.shape, targets.dtype),
            pltpu.SMEM(mask_counts.shape, mask_counts.dtype),
            pltpu.SMEM(answer_lengths.shape, answer_lengths.dtype),
            dma((2, STEPS)), dma((3,)),
            pltpu.VMEM((NZ, vocab_rows // NZ, slots), F32),
            pltpu.VMEM((NZ, vocab_rows // NZ, slots), F32),
            pltpu.VMEM((NZ, 1, slots), F32),
            pltpu.VMEM((lines, LANES), F32),
            pltpu.VMEM((NX * NH, 1, slots), F32),
            pltpu.VMEM((NX * NH, 1, slots), F32),
            pltpu.VMEM((NZ, NY, block, LANES), F32),
            pltpu.VMEM((NZ, 2, max(HALVES_A), LANES), F32),
            pltpu.VMEM((NZ, 3, 2, ROWS_A, LANES), F32),
            pltpu.VMEM((2, ROWS_A, LANES), F32),
            pltpu.VMEM((2, max(HALVES_B), LANES), F32),
            pltpu.VMEM((3, 2, rows_b, LANES), F32),
            pltpu.VMEM((2, NY, rows_b, LANES), F32),
            pltpu.VMEM((block, LANES), F32),
            dma((NX * NH,)), dma((NX * NH,)),
            dma((NX * NH,)), dma((NX * NH,)),
            dma((NZ, NY)), dma((NZ, NY)),
            dma((NZ, 4, 2)), dma((NZ, 4, 2)),
            dma((2,)), dma((2,)),
            dma((4, 2)), dma((4, 2)),
            dma((2, NY)), dma((2, NY)),
        ],
        compiler_params=pltpu.CompilerParams(
            collective_id=0, has_side_effects=True, vmem_limit_bytes=52 * 1024 * 1024
        ),
        cost_estimate=pl.CostEstimate(
            flops=4 * vocab_rows * slots * width,
            bytes_accessed=2 * (vocab_rows + slots) * width,
            transcendentals=vocab_rows * slots,
        ),
        name="head_gradient",
    )(*arguments)
    return seq_loss, head_grad


def solution(mesh):
    return jax.shard_map(
        on_device,
        mesh=mesh,
        in_specs=(P("dp", None), P("vocab", None), P("dp"), P("dp"), P("dp")),
        out_specs=(P("dp"), P(("vocab", "dp"), None)),
        check_vma=False,
    )
```

```python
import jax
import jax.numpy as jnp
from jax import lax
from jax.experimental import pallas as pl
from jax.experimental.pallas import tpu as pltpu
from jax.sharding import PartitionSpec as P

MESH = pl.DeviceIdType.MESH
F32 = jnp.float32

NX, NH = 4, 4
NZ, NY, NC = 3, 8, 2
LANES = 128
STEPS = 4
ROWS_A = 168
HALVES_A, HALVES_B = (88, 80), (56, 64)
DISTANCES = (4, 3, 5, 2, 6, 1, 7, 0)


def toward(way, t):
    return (4 - t if way == 0 else 4 + t) % NY


ORDER = (
    ("product", 1, 0), ("swap", 1, 4), ("product", 1, 1), ("product", 0, 0), ("pair", 1, 4), ("swap", 0, 4),
    ("swap", 1, 5), ("product", 2, 0), ("swap", 1, 6), ("hits_x",), ("swap", 2, 4), ("swap", 1, 3), ("pair", 0, 4),
    ("pair", 1, 5), ("product", 0, 1), ("pair", 2, 4), ("swap", 1, 2), ("pair", 1, 3), ("swap", 0, 2), ("swap", 0, 3),
    ("swap", 0, 5), ("product", 2, 1), ("a", 1, 1, 1), ("swap", 2, 3), ("a", 1, 1, 0), ("pair", 0, 3), ("swap", 0, 6),
    ("swap", 2, 1), ("pair", 0, 5), ("pair", 2, 3), ("swap", 2, 5), ("a", 0, 1, 0), ("swap", 2, 2), ("a", 0, 1, 1),
    ("swap", 1, 0), ("swap", 2, 6), ("zsum", 4), ("swap", 1, 1), ("a", 2, 1, 0), ("pair", 0, 6), ("pair", 2, 5),
    ("swap", 1, 7), ("swap", 2, 7), ("a", 2, 1, 1), ("pair", 1, 2), ("pair", 2, 6), ("pair", 1, 6), ("zsum", 3),
    ("swap", 0, 7), ("pair", 2, 7), ("a", 1, 2, 1), ("a", 1, 2, 0), ("pair", 0, 2), ("pair", 1, 0), ("zsum", 5),
    ("a", 0, 2, 0), ("hits_z",), ("pair", 2, 2), ("swap", 0, 0), ("b", 1, 1), ("a", 0, 2, 1), ("b", 1, 0),
    ("pair", 0, 7), ("pair", 2, 1), ("swap", 0, 1), ("swap", 2, 0), ("pair", 0, 1), ("pair", 1, 1), ("pair", 1, 7),
    ("a", 2, 2, 0), ("a", 2, 2, 1), ("pair", 0, 0), ("a", 1, 3, 0), ("zsum", 6), ("zsum", 2), ("a", 0, 3, 0),
    ("a", 1, 3, 1), ("a", 0, 3, 1), ("b", 2, 0), ("a", 2, 3, 0), ("b", 2, 1), ("loss",), ("a", 2, 3, 1),
    ("a", 1, 4, 1), ("a", 1, 4, 0), ("a", 0, 4, 0), ("pair", 2, 0), ("zsum", 1), ("a", 0, 4, 1), ("zsum", 7),
    ("b", 3, 1), ("b", 3, 0), ("a", 2, 4, 0), ("zsum", 0), ("a", 2, 4, 1), ("sent",), ("end",), ("b", 4, 1),
    ("b", 4, 0),
)


def kernel(hidden_hbm, head_hbm, targets_hbm, counts_hbm, lengths_hbm, out, loss,
           hidden, head, targets, counts, lengths, in_sem, small_sem,
           scores, marks, peaks, grad, stats, hits,
           core_in, ya0, ya, za, yb0, yb, zb, last,
           lse_s, lse_r, hit_s, hit_r, core_s, core_r,
           ya_s, ya_r, za_s, za_r, yb_s, yb_r, zb_s, zb_r):
    vocab_rows, width = head.shape
    slots = hidden.shape[0]
    part = vocab_rows // NZ
    block = vocab_rows * width // LANES // (NZ * NY * NC)
    pitch = width // LANES
    rows_b = block - ROWS_A
    from_a, from_b = (0, HALVES_A[0]), (ROWS_A, ROWS_A + HALVES_B[0])

    v = lax.axis_index("vocab")
    d = lax.axis_index("dp")
    x = v % NX
    h = v // NX
    c = d % NC
    y = (d // NC) % NY
    z = d // (NC * NY)

    partner = d + 1 - 2 * c
    y_next = [(z * NY + (y + 1) % NY) * NC + c, (z * NY + (y + NY - 1) % NY) * NC + c]
    z_peer = [(((z + k) % NZ) * NY + y) * NC + c for k in (1, 2)]
    v_peers = [
        ((h + dh) % NH) * NX + (x + dx) % NX
        for dh in (2, 1, 3, 0) for dx in (2, 1, 3, 0) if dh or dx
    ]

    x_peers = [h * NX + (x + i) % NX for i in range(1, NX)]
    h_peers = [((h + i) % NH) * NX + x for i in range(1, NH)]

    barrier = pltpu.get_barrier_semaphore()
    for peer in v_peers[8:12] + v_peers[:8] + v_peers[12:]:
        pl.semaphore_signal(barrier, inc=1, device_id={"vocab": peer}, device_id_type=MESH)
    seqs = counts.shape[0]
    depth = width // STEPS
    loads = []
    for i in range(STEPS):
        columns = pl.ds(i * depth, depth)
        loads.append((
            pltpu.make_async_copy(hidden_hbm.at[:, columns], hidden.at[:, columns], in_sem.at[0, i]),
            pltpu.make_async_copy(head_hbm.at[:, columns], head.at[:, columns], in_sem.at[1, i]),
        ))
        for load in loads[i]:
            load.start()
    small_loads = [
        pltpu.make_async_copy(targets_hbm, targets, small_sem.at[0]),
        pltpu.make_async_copy(counts_hbm, counts, small_sem.at[1]),
        pltpu.make_async_copy(lengths_hbm, lengths, small_sem.at[2]),
    ]
    for load in small_loads:
        load.start()
    for peer in [partner] + y_next + z_peer:
        pl.semaphore_signal(barrier, inc=1, device_id={"dp": peer}, device_id_type=MESH)

    row = lax.broadcasted_iota(jnp.int32, (part, slots), 0)
    part_lse = []
    for i in range(STEPS):
        for load in loads[i]:
            load.wait()
        columns = pl.ds(i * depth, depth)
        for k in range(NZ):
            value = lax.dot_general(
                head[pl.ds(k * part, part), columns], hidden[:, columns],
                (((1,), (1,)), ((), ())), preferred_element_type=F32,
            )
            if i > 0:
                value = value + scores[k]
            if i == STEPS - 1:
                peak = jnp.max(value, axis=0, keepdims=True)
                marks[k] = value
                value = jnp.exp(value - peak)
                peaks[k] = peak
                part_lse.append(peak + jnp.log(jnp.sum(value, axis=0, keepdims=True)))
            scores[k] = value

    def log_sum_exp(terms):
        top = terms[0]
        for term in terms[1:]:
            top = jnp.maximum(top, term)
        total = jnp.exp(terms[0] - top)
        for term in terms[1:]:
            total = total + jnp.exp(term - top)
        return top + jnp.log(total)

    stats[0] = log_sum_exp(part_lse)

    pl.semaphore_wait(barrier, NX * NH - 1 + 1 + 2 + 2)

    waits = []

    def send(src, dst, send_sem, recv_sem, axis, peer):
        copy = pltpu.make_async_remote_copy(
            src_ref=src, dst_ref=dst, send_sem=send_sem, recv_sem=recv_sem,
            device_id={axis: peer}, device_id_type=MESH,
        )
        copy.start()
        waits.append(copy)
        return copy

    def spread(ref, send_sem, recv_sem, peers, first=0):
        return [
            send(ref.at[first], ref.at[s], send_sem.at[s], recv_sem.at[s], "vocab", peer)
            for s, peer in enumerate(peers, first + 1)
        ]

    def collect(copies, ref, first=0):
        for copy in copies:
            copy.wait_recv()
        return [ref[first + s] for s in range(len(copies) + 1)]

    lse_copies = spread(stats, lse_s, lse_r, v_peers)

    for load in small_loads:
        load.wait()
    position = lax.broadcasted_iota(jnp.int32, (1, slots), 1)
    member, sizes = [], []
    begin = jnp.int32(0)
    weight = jnp.zeros((1, slots), F32)
    for k in range(seqs):
        end_of = begin + counts[k]
        inside = (position >= begin) & (position < end_of)
        member.append(inside)
        sizes.append(jnp.full((1, slots), counts[k], jnp.int32).astype(F32))
        rate = jnp.full((1, slots), lengths[k], jnp.int32).astype(F32) / sizes[k]
        weight = jnp.where(inside, rate, weight)
        begin = end_of

    relative = targets[...].reshape(1, slots) - v * vocab_rows
    own_hit = jnp.zeros((1, slots), F32)
    for k in range(NZ):
        hit = row == relative - k * part
        own_hit += jnp.sum(jnp.where(hit, marks[k], 0.0), axis=0, keepdims=True)
        marks[k] = jnp.where(hit, weight, 0.0)
    hits[0] = own_hit

    log_total = log_sum_exp(collect(lse_copies, stats))

    def line(zo, yo, co):
        return pl.multiple_of(((zo * NY + yo) * NC + co) * block, 8)

    def own(zo, yo, start, count):
        return pl.ds(pl.multiple_of(line(zo, yo, c) + start, 8), count)

    zone = [(z + 1) % NZ, (z + 2) % NZ, z]
    core_copies, ya_copies, za_copies, yb_copies, zb_copies = {}, {}, {}, {}, {}

    def product(k, second):
        zo = zone[k]
        half = part // 2
        start = pl.multiple_of((((y + 4) % NY) // 4 + second) % 2 * half, 8)
        rows = pl.ds(start, half)
        scale = jnp.exp(peaks[zo] - log_total) * weight
        value = (scores[zo, rows, :] * scale - marks[zo, rows, :]).astype(jnp.bfloat16)
        value = jnp.dot(value, hidden[...], preferred_element_type=F32)
        first = (zo * part + start) * pitch
        for j in range(pitch):
            grad[pl.ds(first + j, half, stride=pitch), :] = value[:, j * LANES:(j + 1) * LANES]

    def swap(k, dist):
        i = DISTANCES.index(dist)
        core_copies[k, dist] = send(
            grad.at[pl.ds(line(zone[k], (y + dist) % NY, 1 - c), block)], core_in.at[k, i],
            core_s.at[k, i], core_r.at[k, i], "dp", partner,
        )

    def pair(k, dist):
        yo = (y + dist) % NY
        core_copies[k, dist].wait_recv()
        grad[own(zone[k], yo, 0, block), :] += core_in[k, DISTANCES.index(dist)]
        if dist == 4:
            for way in range(2):
                ya_copies[k, 0, way] = send(
                    grad.at[own(zone[k], yo, from_a[way], HALVES_A[way])],
                    ya0.at[k, way, pl.ds(0, HALVES_A[way])],
                    ya_s.at[k, 0, way], ya_r.at[k, 0, way], "dp", y_next[way],
                )
        if k < 2:
            zb_copies[k, dist] = send(
                grad.at[own(zone[k], yo, ROWS_A, rows_b)], zb.at[k, dist],
                zb_s.at[k, dist], zb_r.at[k, dist], "dp", z_peer[k],
            )

    def a(k, t, way):
        yo = (y + toward(way, t)) % NY
        ya_copies[k, t - 1, way].wait_recv()
        if t == 1:
            grad[own(zone[k], yo, from_a[way], HALVES_A[way]), :] += ya0[k, way, pl.ds(0, HALVES_A[way]), :]
        else:
            grad[own(zone[k], yo, 0, ROWS_A), :] += ya[k, t - 2, way]
        if t < 4:
            ya_copies[k, t, way] = send(
                grad.at[own(zone[k], yo, 0, ROWS_A)], ya.at[k, t - 1, way],
                ya_s.at[k, t, way], ya_r.at[k, t, way], "dp", y_next[way],
            )
            return
        closed.append((k, way))
        if k < 2 and (k, 1 - way) in closed:
            za_copies[k] = send(
                grad.at[own(zone[k], y, 0, ROWS_A)], za.at[k], za_s.at[k], za_r.at[k], "dp", z_peer[k]
            )

    closed = []

    def zsum(dist):
        yo = (y + dist) % NY
        for k in range(2):
            zb_copies[k, dist].wait_recv()
        grad[own(z, yo, ROWS_A, rows_b), :] += zb[0, dist] + zb[1, dist]
        if dist == 4:
            for way in range(2):
                yb_copies[0, way] = send(
                    grad.at[own(z, yo, from_b[way], HALVES_B[way])],
                    yb0.at[way, pl.ds(0, HALVES_B[way])],
                    yb_s.at[0, way], yb_r.at[0, way], "dp", y_next[way],
                )

    def b(t, way):
        yo = (y + toward(way, t)) % NY
        yb_copies[t - 1, way].wait_recv()
        if t == 1:
            grad[own(z, yo, from_b[way], HALVES_B[way]), :] += yb0[way, pl.ds(0, HALVES_B[way]), :]
        else:
            grad[own(z, yo, ROWS_A, rows_b), :] += yb[t - 2, way]
        if t < 4:
            yb_copies[t, way] = send(
                grad.at[own(z, yo, ROWS_A, rows_b)], yb.at[t - 1, way],
                yb_s.at[t, way], yb_r.at[t, way], "dp", y_next[way],
            )

    def end():
        for k in range(2):
            za_copies[k].wait_recv()
        last[pl.ds(0, ROWS_A), :] = grad[own(z, y, 0, ROWS_A), :] + za[0] + za[1]

    hit_copies = []

    def hits_x():
        hit_copies.extend(spread(hits, hit_s, hit_r, x_peers))

    def hits_z():
        hits[NX] = sum(collect(hit_copies, hits))
        hit_copies[:] = spread(hits, hit_s, hit_r, h_peers, NX)

    def finish_loss():
        target_logit = sum(collect(hit_copies, hits, NX))
        cross = log_total - target_logit
        for k in range(seqs):
            mean = jnp.where(member[k], cross, 0.0) / sizes[k]
            loss[k] = jnp.sum(mean)

    def sent():
        for copy in waits[:-16]:
            copy.wait_send()
        del waits[:-16]

    steps = {"product": product, "swap": swap, "pair": pair, "a": a, "zsum": zsum, "b": b, "end": end,
             "hits_x": hits_x, "hits_z": hits_z, "loss": finish_loss, "sent": sent}
    for kind, *where in ORDER:
        steps[kind](*where)

    last[pl.ds(ROWS_A, rows_b), :] = grad[own(z, y, ROWS_A, rows_b), :]
    for j in range(pitch):
        out[:, j * LANES:(j + 1) * LANES] = last[pl.ds(j, out.shape[0], stride=pitch), :]

    for copy in waits:
        copy.wait_send()


def on_device(hidden, head, targets, mask_counts, answer_lengths):
    vocab_rows, width = head.shape
    slots = hidden.shape[0]
    lines = vocab_rows * width // LANES
    block = lines // (NZ * NY * NC)
    rows_b = block - ROWS_A
    anywhere = pl.BlockSpec(memory_space=pltpu.HBM)
    vmem = pl.BlockSpec(memory_space=pltpu.VMEM)
    smem = pl.BlockSpec(memory_space=pltpu.SMEM)
    dma = pltpu.SemaphoreType.DMA
    arguments = [
        pltpu.with_memory_space_constraint(argument, pltpu.HBM)
        for argument in (hidden, head, targets, mask_counts, answer_lengths)
    ]
    head_grad, seq_loss = pl.pallas_call(
        kernel,
        out_shape=(
            jax.ShapeDtypeStruct((vocab_rows // (NZ * NY * NC), width), F32),
            jax.ShapeDtypeStruct(mask_counts.shape, F32),
        ),
        in_specs=[anywhere] * 5,
        out_specs=(vmem, smem),
        scratch_shapes=[
            pltpu.VMEM(hidden.shape, hidden.dtype),
            pltpu.VMEM(head.shape, head.dtype),
            pltpu.VMEM(targets.shape, targets.dtype),
            pltpu.SMEM(mask_counts.shape, mask_counts.dtype),
            pltpu.SMEM(answer_lengths.shape, answer_lengths.dtype),
            dma((2, STEPS)), dma((3,)),
            pltpu.VMEM((NZ, vocab_rows // NZ, slots), F32),
            pltpu.VMEM((NZ, vocab_rows // NZ, slots), F32),
            pltpu.VMEM((NZ, 1, slots), F32),
            pltpu.VMEM((lines, LANES), F32),
            pltpu.VMEM((NX * NH, 1, slots), F32),
            pltpu.VMEM((NX + NH, 1, slots), F32),
            pltpu.VMEM((NZ, NY, block, LANES), F32),
            pltpu.VMEM((NZ, 2, max(HALVES_A), LANES), F32),
            pltpu.VMEM((NZ, 3, 2, ROWS_A, LANES), F32),
            pltpu.VMEM((2, ROWS_A, LANES), F32),
            pltpu.VMEM((2, max(HALVES_B), LANES), F32),
            pltpu.VMEM((3, 2, rows_b, LANES), F32),
            pltpu.VMEM((2, NY, rows_b, LANES), F32),
            pltpu.VMEM((block, LANES), F32),
            dma((NX * NH,)), dma((NX * NH,)),
            dma((NX + NH,)), dma((NX + NH,)),
            dma((NZ, NY)), dma((NZ, NY)),
            dma((NZ, 4, 2)), dma((NZ, 4, 2)),
            dma((2,)), dma((2,)),
            dma((4, 2)), dma((4, 2)),
            dma((2, NY)), dma((2, NY)),
        ],
        compiler_params=pltpu.CompilerParams(
            collective_id=0, has_side_effects=True, vmem_limit_bytes=52 * 1024 * 1024
        ),
        cost_estimate=pl.CostEstimate(
            flops=4 * vocab_rows * slots * width,
            bytes_accessed=2 * (vocab_rows + slots) * width,
            transcendentals=vocab_rows * slots,
        ),
        name="head_gradient",
    )(*arguments)
    return seq_loss, head_grad


def solution(mesh):
    return jax.shard_map(
        on_device,
        mesh=mesh,
        in_specs=(P("dp", None), P("vocab", None), P("dp"), P("dp"), P("dp")),
        out_specs=(P("dp"), P(("vocab", "dp"), None)),
        check_vma=False,
    )
```

```python
import jax
import jax.numpy as jnp
from jax import lax
from jax.experimental import pallas as pl
from jax.experimental.pallas import tpu as pltpu
from jax.sharding import PartitionSpec as P

MESH = pl.DeviceIdType.MESH
F32 = jnp.float32

NX, NH = 4, 4
NZ, NY, NC = 3, 8, 2
LANES = 128
STEPS = 4
ROWS_A = 168
HALVES_A, HALVES_B = (88, 80), (56, 64)
DISTANCES = (4, 3, 5, 2, 6, 1, 7, 0)


def toward(way, t):
    return (4 - t if way == 0 else 4 + t) % NY


ORDER = (
    ("product", 1, 0), ("swap", 1, 4), ("product", 1, 1), ("product", 0, 0), ("pair", 1, 4), ("swap", 0, 4),
    ("swap", 1, 5), ("product", 2, 0), ("swap", 1, 6), ("hits_x",), ("swap", 2, 4), ("swap", 1, 3), ("pair", 0, 4),
    ("pair", 1, 5), ("product", 0, 1), ("pair", 2, 4), ("swap", 1, 2), ("pair", 1, 3), ("swap", 0, 2), ("swap", 0, 3),
    ("swap", 0, 5), ("product", 2, 1), ("a", 1, 1, 1), ("swap", 2, 3), ("a", 1, 1, 0), ("pair", 0, 3), ("swap", 0, 6),
    ("swap", 2, 1), ("pair", 0, 5), ("pair", 2, 3), ("swap", 2, 5), ("a", 0, 1, 0), ("swap", 2, 2), ("a", 0, 1, 1),
    ("swap", 1, 0), ("swap", 2, 6), ("zsum", 4), ("swap", 1, 1), ("a", 2, 1, 0), ("pair", 0, 6), ("pair", 2, 5),
    ("swap", 1, 7), ("swap", 2, 7), ("a", 2, 1, 1), ("pair", 1, 2), ("pair", 2, 6), ("pair", 1, 6), ("zsum", 3),
    ("swap", 0, 7), ("pair", 2, 7), ("a", 1, 2, 1), ("a", 1, 2, 0), ("pair", 0, 2), ("pair", 1, 0), ("zsum", 5),
    ("a", 0, 2, 0), ("hits_z",), ("pair", 2, 2), ("swap", 0, 0), ("b", 1, 1), ("a", 0, 2, 1), ("b", 1, 0),
    ("pair", 0, 7), ("pair", 2, 1), ("swap", 0, 1), ("swap", 2, 0), ("pair", 0, 1), ("pair", 1, 1), ("pair", 1, 7),
    ("a", 2, 2, 0), ("a", 2, 2, 1), ("pair", 0, 0), ("a", 1, 3, 0), ("zsum", 6), ("zsum", 2), ("a", 0, 3, 0),
    ("a", 1, 3, 1), ("a", 0, 3, 1), ("b", 2, 0), ("a", 2, 3, 0), ("b", 2, 1), ("loss",), ("a", 2, 3, 1),
    ("a", 1, 4, 1), ("a", 1, 4, 0), ("a", 0, 4, 0), ("pair", 2, 0), ("zsum", 1), ("a", 0, 4, 1), ("zsum", 7),
    ("b", 3, 1), ("b", 3, 0), ("a", 2, 4, 0), ("zsum", 0), ("a", 2, 4, 1), ("sent",), ("end",), ("sent", 6),
    ("b", 4, 1), ("b", 4, 0),
)


def kernel(hidden_hbm, head_hbm, targets_hbm, counts_hbm, lengths_hbm, out, loss,
           hidden, head, targets, counts, lengths, in_sem, small_sem,
           scores, marks, peaks, grad, stats, hits,
           core_in, ya0, ya, za, yb0, yb, zb, last,
           lse_s, lse_r, hit_s, hit_r, core_s, core_r,
           ya_s, ya_r, za_s, za_r, yb_s, yb_r, zb_s, zb_r):
    vocab_rows, width = head.shape
    slots = hidden.shape[0]
    part = vocab_rows // NZ
    block = vocab_rows * width // LANES // (NZ * NY * NC)
    pitch = width // LANES
    rows_b = block - ROWS_A
    from_a, from_b = (0, HALVES_A[0]), (ROWS_A, ROWS_A + HALVES_B[0])

    v = lax.axis_index("vocab")
    d = lax.axis_index("dp")
    x = v % NX
    h = v // NX
    c = d % NC
    y = (d // NC) % NY
    z = d // (NC * NY)

    partner = d + 1 - 2 * c
    y_next = [(z * NY + (y + 1) % NY) * NC + c, (z * NY + (y + NY - 1) % NY) * NC + c]
    z_peer = [(((z + k) % NZ) * NY + y) * NC + c for k in (1, 2)]
    v_peers = [
        ((h + dh) % NH) * NX + (x + dx) % NX
        for dh in (2, 1, 3, 0) for dx in (2, 1, 3, 0) if dh or dx
    ]

    x_peers = [h * NX + (x + i) % NX for i in range(1, NX)]
    h_peers = [((h + i) % NH) * NX + x for i in range(1, NH)]

    barrier = pltpu.get_barrier_semaphore()
    for peer in v_peers[8:12] + v_peers[:8] + v_peers[12:]:
        pl.semaphore_signal(barrier, inc=1, device_id={"vocab": peer}, device_id_type=MESH)
    seqs = counts.shape[0]
    depth = width // STEPS
    loads = []
    for i in range(STEPS):
        columns = pl.ds(i * depth, depth)
        loads.append((
            pltpu.make_async_copy(hidden_hbm.at[:, columns], hidden.at[:, columns], in_sem.at[0, i]),
            pltpu.make_async_copy(head_hbm.at[:, columns], head.at[:, columns], in_sem.at[1, i]),
        ))
        for load in loads[i]:
            load.start()
    small_loads = [
        pltpu.make_async_copy(targets_hbm, targets, small_sem.at[0]),
        pltpu.make_async_copy(counts_hbm, counts, small_sem.at[1]),
        pltpu.make_async_copy(lengths_hbm, lengths, small_sem.at[2]),
    ]
    for load in small_loads:
        load.start()
    for peer in [partner] + y_next + z_peer:
        pl.semaphore_signal(barrier, inc=1, device_id={"dp": peer}, device_id_type=MESH)

    row = lax.broadcasted_iota(jnp.int32, (part, slots), 0)
    part_lse = []
    for i in range(STEPS):
        for load in loads[i]:
            load.wait()
        columns = pl.ds(i * depth, depth)
        for k in range(NZ):
            value = lax.dot_general(
                head[pl.ds(k * part, part), columns], hidden[:, columns],
                (((1,), (1,)), ((), ())), preferred_element_type=F32,
            )
            if i > 0:
                value = value + scores[k]
            if i == STEPS - 1:
                peak = jnp.max(value, axis=0, keepdims=True)
                marks[k] = value
                value = jnp.exp(value - peak)
                peaks[k] = peak
                part_lse.append(peak + jnp.log(jnp.sum(value, axis=0, keepdims=True)))
            scores[k] = value

    def log_sum_exp(terms):
        top = terms[0]
        for term in terms[1:]:
            top = jnp.maximum(top, term)
        total = jnp.exp(terms[0] - top)
        for term in terms[1:]:
            total = total + jnp.exp(term - top)
        return top + jnp.log(total)

    stats[0] = log_sum_exp(part_lse)

    pl.semaphore_wait(barrier, NX * NH - 1 + 1 + 2 + 2)

    waits = []

    def send(src, dst, send_sem, recv_sem, axis, peer):
        copy = pltpu.make_async_remote_copy(
            src_ref=src, dst_ref=dst, send_sem=send_sem, recv_sem=recv_sem,
            device_id={axis: peer}, device_id_type=MESH,
        )
        copy.start()
        waits.append(copy)
        return copy

    def spread(ref, send_sem, recv_sem, peers, first=0):
        return [
            send(ref.at[first], ref.at[s], send_sem.at[s], recv_sem.at[s], "vocab", peer)
            for s, peer in enumerate(peers, first + 1)
        ]

    def collect(copies, ref, first=0):
        for copy in copies:
            copy.wait_recv()
        return [ref[first + s] for s in range(len(copies) + 1)]

    lse_copies = spread(stats, lse_s, lse_r, v_peers)

    for load in small_loads:
        load.wait()
    position = lax.broadcasted_iota(jnp.int32, (1, slots), 1)
    member, sizes = [], []
    begin = jnp.int32(0)
    weight = jnp.zeros((1, slots), F32)
    for k in range(seqs):
        end_of = begin + counts[k]
        inside = (position >= begin) & (position < end_of)
        member.append(inside)
        sizes.append(jnp.full((1, slots), counts[k], jnp.int32).astype(F32))
        rate = jnp.full((1, slots), lengths[k], jnp.int32).astype(F32) / sizes[k]
        weight = jnp.where(inside, rate, weight)
        begin = end_of

    relative = targets[...].reshape(1, slots) - v * vocab_rows
    own_hit = jnp.zeros((1, slots), F32)
    for k in range(NZ):
        hit = row == relative - k * part
        own_hit += jnp.sum(jnp.where(hit, marks[k], 0.0), axis=0, keepdims=True)
        marks[k] = jnp.where(hit, weight, 0.0)
    hits[0] = own_hit

    log_total = log_sum_exp(collect(lse_copies, stats))

    def line(zo, yo, co):
        return pl.multiple_of(((zo * NY + yo) * NC + co) * block, 8)

    def own(zo, yo, start, count):
        return pl.ds(pl.multiple_of(line(zo, yo, c) + start, 8), count)

    zone = [(z + 1) % NZ, (z + 2) % NZ, z]
    core_copies, ya_copies, za_copies, yb_copies, zb_copies = {}, {}, {}, {}, {}

    def product(k, second):
        zo = zone[k]
        half = part // 2
        start = pl.multiple_of((((y + 4) % NY) // 4 + second) % 2 * half, 8)
        rows = pl.ds(start, half)
        scale = jnp.exp(peaks[zo] - log_total) * weight
        value = (scores[zo, rows, :] * scale - marks[zo, rows, :]).astype(jnp.bfloat16)
        value = jnp.dot(value, hidden[...], preferred_element_type=F32)
        first = (zo * part + start) * pitch
        for j in range(pitch):
            grad[pl.ds(first + j, half, stride=pitch), :] = value[:, j * LANES:(j + 1) * LANES]

    def swap(k, dist):
        i = DISTANCES.index(dist)
        core_copies[k, dist] = send(
            grad.at[pl.ds(line(zone[k], (y + dist) % NY, 1 - c), block)], core_in.at[k, i],
            core_s.at[k, i], core_r.at[k, i], "dp", partner,
        )

    def pair(k, dist):
        yo = (y + dist) % NY
        core_copies[k, dist].wait_recv()
        grad[own(zone[k], yo, 0, block), :] += core_in[k, DISTANCES.index(dist)]
        if dist == 4:
            for way in range(2):
                ya_copies[k, 0, way] = send(
                    grad.at[own(zone[k], yo, from_a[way], HALVES_A[way])],
                    ya0.at[k, way, pl.ds(0, HALVES_A[way])],
                    ya_s.at[k, 0, way], ya_r.at[k, 0, way], "dp", y_next[way],
                )
        if k < 2:
            zb_copies[k, dist] = send(
                grad.at[own(zone[k], yo, ROWS_A, rows_b)], zb.at[k, dist],
                zb_s.at[k, dist], zb_r.at[k, dist], "dp", z_peer[k],
            )

    def a(k, t, way):
        yo = (y + toward(way, t)) % NY
        ya_copies[k, t - 1, way].wait_recv()
        if t == 1:
            grad[own(zone[k], yo, from_a[way], HALVES_A[way]), :] += ya0[k, way, pl.ds(0, HALVES_A[way]), :]
        else:
            grad[own(zone[k], yo, 0, ROWS_A), :] += ya[k, t - 2, way]
        if t < 4:
            ya_copies[k, t, way] = send(
                grad.at[own(zone[k], yo, 0, ROWS_A)], ya.at[k, t - 1, way],
                ya_s.at[k, t, way], ya_r.at[k, t, way], "dp", y_next[way],
            )
            return
        closed.append((k, way))
        if k < 2 and (k, 1 - way) in closed:
            za_copies[k] = send(
                grad.at[own(zone[k], y, 0, ROWS_A)], za.at[k], za_s.at[k], za_r.at[k], "dp", z_peer[k]
            )

    closed = []

    def zsum(dist):
        yo = (y + dist) % NY
        for k in range(2):
            zb_copies[k, dist].wait_recv()
        grad[own(z, yo, ROWS_A, rows_b), :] += zb[0, dist] + zb[1, dist]
        if dist == 4:
            for way in range(2):
                yb_copies[0, way] = send(
                    grad.at[own(z, yo, from_b[way], HALVES_B[way])],
                    yb0.at[way, pl.ds(0, HALVES_B[way])],
                    yb_s.at[0, way], yb_r.at[0, way], "dp", y_next[way],
                )

    def b(t, way):
        yo = (y + toward(way, t)) % NY
        yb_copies[t - 1, way].wait_recv()
        if t == 1:
            grad[own(z, yo, from_b[way], HALVES_B[way]), :] += yb0[way, pl.ds(0, HALVES_B[way]), :]
        else:
            grad[own(z, yo, ROWS_A, rows_b), :] += yb[t - 2, way]
        if t < 4:
            yb_copies[t, way] = send(
                grad.at[own(z, yo, ROWS_A, rows_b)], yb.at[t - 1, way],
                yb_s.at[t, way], yb_r.at[t, way], "dp", y_next[way],
            )

    def end():
        for k in range(2):
            za_copies[k].wait_recv()
        last[pl.ds(0, ROWS_A), :] = grad[own(z, y, 0, ROWS_A), :] + za[0] + za[1]

    hit_copies = []

    def hits_x():
        hit_copies.extend(spread(hits, hit_s, hit_r, x_peers))

    def hits_z():
        hits[NX] = sum(collect(hit_copies, hits))
        hit_copies[:] = spread(hits, hit_s, hit_r, h_peers, NX)

    def finish_loss():
        target_logit = sum(collect(hit_copies, hits, NX))
        cross = log_total - target_logit
        for k in range(seqs):
            mean = jnp.where(member[k], cross, 0.0) / sizes[k]
            loss[k] = jnp.sum(mean)

    def sent(kept=16):
        for copy in waits[:-kept]:
            copy.wait_send()
        del waits[:-kept]

    steps = {"product": product, "swap": swap, "pair": pair, "a": a, "zsum": zsum, "b": b, "end": end,
             "hits_x": hits_x, "hits_z": hits_z, "loss": finish_loss, "sent": sent}
    for kind, *where in ORDER:
        steps[kind](*where)

    last[pl.ds(ROWS_A, rows_b), :] = grad[own(z, y, ROWS_A, rows_b), :]
    for j in range(pitch):
        out[:, j * LANES:(j + 1) * LANES] = last[pl.ds(j, out.shape[0], stride=pitch), :]

    for copy in waits:
        copy.wait_send()


def on_device(hidden, head, targets, mask_counts, answer_lengths):
    vocab_rows, width = head.shape
    slots = hidden.shape[0]
    lines = vocab_rows * width // LANES
    block = lines // (NZ * NY * NC)
    rows_b = block - ROWS_A
    anywhere = pl.BlockSpec(memory_space=pltpu.HBM)
    vmem = pl.BlockSpec(memory_space=pltpu.VMEM)
    smem = pl.BlockSpec(memory_space=pltpu.SMEM)
    dma = pltpu.SemaphoreType.DMA
    arguments = [
        pltpu.with_memory_space_constraint(argument, pltpu.HBM)
        for argument in (hidden, head, targets, mask_counts, answer_lengths)
    ]
    head_grad, seq_loss = pl.pallas_call(
        kernel,
        out_shape=(
            jax.ShapeDtypeStruct((vocab_rows // (NZ * NY * NC), width), F32),
            jax.ShapeDtypeStruct(mask_counts.shape, F32),
        ),
        in_specs=[anywhere] * 5,
        out_specs=(vmem, smem),
        scratch_shapes=[
            pltpu.VMEM(hidden.shape, hidden.dtype),
            pltpu.VMEM(head.shape, head.dtype),
            pltpu.VMEM(targets.shape, targets.dtype),
            pltpu.SMEM(mask_counts.shape, mask_counts.dtype),
            pltpu.SMEM(answer_lengths.shape, answer_lengths.dtype),
            dma((2, STEPS)), dma((3,)),
            pltpu.VMEM((NZ, vocab_rows // NZ, slots), F32),
            pltpu.VMEM((NZ, vocab_rows // NZ, slots), F32),
            pltpu.VMEM((NZ, 1, slots), F32),
            pltpu.VMEM((lines, LANES), F32),
            pltpu.VMEM((NX * NH, 1, slots), F32),
            pltpu.VMEM((NX + NH, 1, slots), F32),
            pltpu.VMEM((NZ, NY, block, LANES), F32),
            pltpu.VMEM((NZ, 2, max(HALVES_A), LANES), F32),
            pltpu.VMEM((NZ, 3, 2, ROWS_A, LANES), F32),
            pltpu.VMEM((2, ROWS_A, LANES), F32),
            pltpu.VMEM((2, max(HALVES_B), LANES), F32),
            pltpu.VMEM((3, 2, rows_b, LANES), F32),
            pltpu.VMEM((2, NY, rows_b, LANES), F32),
            pltpu.VMEM((block, LANES), F32),
            dma((NX * NH,)), dma((NX * NH,)),
            dma((NX + NH,)), dma((NX + NH,)),
            dma((NZ, NY)), dma((NZ, NY)),
            dma((NZ, 4, 2)), dma((NZ, 4, 2)),
            dma((2,)), dma((2,)),
            dma((4, 2)), dma((4, 2)),
            dma((2, NY)), dma((2, NY)),
        ],
        compiler_params=pltpu.CompilerParams(
            collective_id=0, has_side_effects=True, vmem_limit_bytes=52 * 1024 * 1024
        ),
        cost_estimate=pl.CostEstimate(
            flops=4 * vocab_rows * slots * width,
            bytes_accessed=2 * (vocab_rows + slots) * width,
            transcendentals=vocab_rows * slots,
        ),
        name="head_gradient",
    )(*arguments)
    return seq_loss, head_grad


def solution(mesh):
    return jax.shard_map(
        on_device,
        mesh=mesh,
        in_specs=(P("dp", None), P("vocab", None), P("dp"), P("dp"), P("dp")),
        out_specs=(P("dp"), P(("vocab", "dp"), None)),
        check_vma=False,
    )
```
